128 devices in a mesh: section: 2 (over x_hi), ctx: 16 (over z, x_lo, core), fsdp: 4 (over y).
Axes of the slice: x: 4 (x_hi: 2, x_lo: 2; x = x_hi * 2 + x_lo), y: 4, z: 4, core: 2. Of those that a mesh axis runs over, the one named last changes fastest.
Arguments:
- tokens: bfloat16 [2, 4, 2, 768, 960], P(None, 'fsdp', None, 'ctx'), may hold values from -6 to 6
- cotangent: bfloat16 [2, 4, 2, 768, 960], P(None, 'fsdp', None, 'ctx'), may hold values from -6 to 6
- norm_attn: bfloat16 [2, 960], P('section', 'fsdp'), may hold values from 0.25 to 1.75
- w_query: bfloat16 [2, 960, 960], P('section', 'fsdp'), may hold values from -0.1875 to 0.1875
- key_projection: bfloat16 [2, 960, 320], P('section', 'fsdp'), may hold values from -0.1875 to 0.1875
- value_projection: bfloat16 [2, 960, 320], P('section', 'fsdp'), may hold values from -0.1875 to 0.1875
- w_out: bfloat16 [2, 960, 960], P('section', 'fsdp'), may hold values from -3.5 to 3.5
- norm_ffn: bfloat16 [2, 960], P('section', 'fsdp'), may hold values from 0.25 to 1.75
- w_gate: bfloat16 [2, 960, 2560], P('section', 'fsdp'), may hold values from -0.1875 to 0.1875
- w_up: bfloat16 [2, 960, 2560], P('section', 'fsdp'), may hold values from -0.1875 to 0.1875
- w_down: bfloat16 [2, 2560, 960], P('section', 'fsdp'), may hold values from -0.125 to 0.125
Outputs:
- acts: bfloat16 [2, 2, 4, 2, 768, 960], P('section', None, 'fsdp', None, 'ctx')
- in_grads: float32 [2, 2, 4, 2, 768, 960], P('section', None, 'fsdp', None, 'ctx')
- grad_norm_attn: float32 [2, 960], P('section', 'fsdp')
- grad_query: float32 [2, 960, 960], P('section', 'fsdp')
- grad_key: float32 [2, 960, 320], P('section', 'fsdp')
- grad_value: float32 [2, 960, 320], P('section', 'fsdp')
- grad_out: float32 [2, 960, 960], P('section', 'fsdp')
- grad_norm_ffn: float32 [2, 960], P('section', 'fsdp')
- grad_gate: float32 [2, 960, 2560], P('section', 'fsdp')
- grad_up: float32 [2, 960, 2560], P('section', 'fsdp')
- grad_down: float32 [2, 2560, 960], P('section', 'fsdp')
The draws below stay inside these ranges and needn't reach their ends.
All inputs are finite; a program needn't handle non-finite values.
Results may differ from the reference program's by a relative error of at most 0.03.
Values may be sent and summed in bfloat16 or wider, within the bound.
No kernel may reach another device: no remote copies, remote signals or barrier semaphores. Data moves between devices by JAX's collectives and lax.ppermute only.
A program may use at most 192 MiB of HBM per device.

```python
import math
import jax
import jax.numpy as jnp
from jax import lax

MODEL_DIMENSION = 960
QUERY_HEADS = 15
KEY_VALUE_HEADS = 5
HEAD_DIMENSION = 64
FF = 2560
MICRO = 2
LENGTH = 1536
BLK = 48
SEQS = 4
N_SECTION = 2
N_CTX = 16


def block_levels(rng, dims, pieces, low, top_value):
    def one(dim, parts):
        steps = jax.random.uniform(jax.random.fold_in(jax.random.fold_in(rng, 6), dim), (parts,), jnp.float32, low / len(pieces), top_value / len(pieces))
        return jnp.repeat(jnp.exp(steps), dims[dim] // parts).reshape((-1,) + (1,) * (len(dims) - dim - 1))

    level = one(*pieces[0])
    for cut in pieces[1:]:
        level = level * one(*cut)
    return level


def centred(rng, extent, spread, reach, shards=(), kind=jnp.bfloat16):
    result = spread * jax.random.normal(rng, extent, jnp.float32)
    if shards:
        result = result * block_levels(rng, extent, shards, -0.22, 0.18)
    return jnp.clip(result, -reach, reach).astype(kind)


def setup_inputs(seed: int = 0) -> dict:
    seeds = jax.random.split(jax.random.key(seed), 12)
    tokens = centred(seeds[0], (MICRO, SEQS, 2, LENGTH // 2, MODEL_DIMENSION), 1.0, 6.0, ((1, 4), (3, 16)))
    cotangent = centred(seeds[1], (MICRO, SEQS, 2, LENGTH // 2, MODEL_DIMENSION), 1.0, 6.0, ((1, 4), (3, 16)))
    norm_attn = jnp.clip(1.0 + 0.15 * jax.random.normal(seeds[2], (N_SECTION, MODEL_DIMENSION), jnp.float32), 0.25, 1.75).astype(jnp.bfloat16)
    w_query = centred(seeds[3], (N_SECTION, MODEL_DIMENSION, QUERY_HEADS * HEAD_DIMENSION), MODEL_DIMENSION ** -0.5, 0.1875, ((0, 2), (1, 4)))
    key_projection = centred(seeds[4], (N_SECTION, MODEL_DIMENSION, KEY_VALUE_HEADS * HEAD_DIMENSION), MODEL_DIMENSION ** -0.5, 0.1875, ((0, 2), (1, 4)))
    value_projection = centred(seeds[5], (N_SECTION, MODEL_DIMENSION, KEY_VALUE_HEADS * HEAD_DIMENSION), MODEL_DIMENSION ** -0.5, 0.1875, ((0, 2), (1, 4)))
    w_out = centred(seeds[6], (N_SECTION, QUERY_HEADS * HEAD_DIMENSION, MODEL_DIMENSION), (max(1, QUERY_HEADS * HEAD_DIMENSION // 256)) ** -0.5, 3.5, ((0, 2), (1, 4)))
    norm_ffn = jnp.clip(1.0 + 0.15 * jax.random.normal(seeds[7], (N_SECTION, MODEL_DIMENSION), jnp.float32), 0.25, 1.75).astype(jnp.bfloat16)
    w_gate = centred(seeds[8], (N_SECTION, MODEL_DIMENSION, FF), MODEL_DIMENSION ** -0.5, 0.1875, ((0, 2), (1, 4)))
    w_up = centred(seeds[9], (N_SECTION, MODEL_DIMENSION, FF), MODEL_DIMENSION ** -0.5, 0.1875, ((0, 2), (1, 4)))
    w_down = centred(seeds[10], (N_SECTION, FF, MODEL_DIMENSION), FF ** -0.5, 0.125, ((0, 2), (1, 4)))
    return dict(tokens=tokens, cotangent=cotangent, norm_attn=norm_attn, w_query=w_query, key_projection=key_projection, value_projection=value_projection, w_out=w_out, norm_ffn=norm_ffn, w_gate=w_gate, w_up=w_up, w_down=w_down)


EPSILON = 1e-05
THETA = 10000.0
MASKED = -1e+30

@jax.custom_vjp
def lower_precision(v):
    return lax.optimization_barrier(v.astype(jnp.bfloat16)).astype(jnp.float32)

@jax.custom_vjp
def lower_precision_back(v):
    return v

def low_keep(v):
    return (lower_precision(v), None)

def low_pass(kept, grad):
    return (grad,)

def back_keep(v):
    return (v, None)

def back_low(kept, grad):
    return (lower_precision(grad),)
lower_precision.defvjp(low_keep, low_pass)
lower_precision_back.defvjp(back_keep, back_low)

def matrix_product(left_side, right_side):
    return jnp.dot(left_side, right_side, precision=lax.Precision.HIGHEST, preferred_element_type=jnp.float32)

def rotary_tables(positions, head_size):
    half_size = head_size // 2
    inverse = THETA ** (-(jnp.arange(half_size, dtype=jnp.float32) * 2.0) / head_size)
    angles = positions.astype(jnp.float32)[:, None] * inverse[None, :]
    return (jnp.cos(angles), jnp.sin(angles))

def apply_rotary(values, cosine_rows_table, sine):
    half_size = values.shape[-1] // 2
    first_half = values[..., :half_size]
    second_half = values[..., half_size:]
    cos_rows = cosine_rows_table[:, None, :]
    sin_rows = sine[:, None, :]
    return jnp.concatenate([first_half * cos_rows - second_half * sin_rows, second_half * cos_rows + first_half * sin_rows], axis=-1)

def rms_scale(values, gain):
    return values * lax.rsqrt(lax.optimization_barrier(jnp.mean(values * values, axis=-1, keepdims=True)) + EPSILON) * gain

def layer(inputs, positions, params):
    norm_gain, query_weight, key_matrix, value_matrix, out_weight, ffn_gain, gate_weight, up_weight, down_weight = params
    sequence_length = inputs.shape[0]
    query_group_count = QUERY_HEADS // KEY_VALUE_HEADS
    head_scale_factor = 1.0 / math.sqrt(HEAD_DIMENSION)
    cosine_rows_table, sine_rows_table = rotary_tables(positions, HEAD_DIMENSION)
    normalized_input = lower_precision(rms_scale(inputs, norm_gain))
    query_rows = lower_precision_back(matrix_product(normalized_input, query_weight)).reshape(sequence_length, QUERY_HEADS, HEAD_DIMENSION)
    key_row_block = lower_precision_back(matrix_product(normalized_input, key_matrix)).reshape(sequence_length, KEY_VALUE_HEADS, HEAD_DIMENSION)
    value_row_block = lower_precision(lower_precision_back(matrix_product(normalized_input, value_matrix))).reshape(sequence_length, KEY_VALUE_HEADS, HEAD_DIMENSION)
    query_rows = lower_precision(apply_rotary(query_rows, cosine_rows_table, sine_rows_table) * head_scale_factor).reshape(sequence_length, KEY_VALUE_HEADS, query_group_count, HEAD_DIMENSION)
    key_row_block = lower_precision(apply_rotary(key_row_block, cosine_rows_table, sine_rows_table))
    block = math.gcd(sequence_length, 512)

    def attend(start):
        query_block = lax.dynamic_slice_in_dim(query_rows, start, block, 0)
        row_positions = lax.dynamic_slice_in_dim(positions, start, block, 0)
        scores = jnp.einsum('qgrd,kgd->grqk', query_block, key_row_block, precision=lax.Precision.HIGHEST)
        scores = lower_precision_back(scores)
        allowed = positions[None, :] <= row_positions[:, None]
        scores = jnp.where(allowed, scores, MASKED)
        row_max = lax.optimization_barrier(jnp.max(scores, axis=-1, keepdims=True))
        weights = jnp.exp(scores - row_max)
        weights_low = lower_precision(weights / lax.optimization_barrier(jnp.sum(weights, axis=-1, keepdims=True)))
        return jnp.einsum('grqk,kgd->qgrd', weights_low, value_row_block, precision=lax.Precision.HIGHEST)
    starts = jnp.arange(sequence_length // block, dtype=jnp.int32) * block
    attended = lax.map(jax.checkpoint(attend), starts).reshape(sequence_length, QUERY_HEADS * HEAD_DIMENSION)
    attended = lower_precision(lower_precision_back(attended))
    mixed_rows = inputs + lower_precision_back(matrix_product(attended, out_weight))
    normed_ffn = lower_precision(rms_scale(mixed_rows, ffn_gain))
    gate_value = lower_precision_back(matrix_product(normed_ffn, gate_weight))
    up_value = lower_precision_back(matrix_product(normed_ffn, up_weight))
    hidden = lower_precision(jax.nn.silu(gate_value) * up_value)
    return mixed_rows + lower_precision_back(matrix_product(hidden, down_weight))

def reference(tokens, cotangent, norm_attn, w_query, key_projection, value_projection, w_out, norm_ffn, w_gate, w_up, w_down):
    half_index = jnp.arange(LENGTH // 2, dtype=jnp.int32)
    block_index = half_index // BLK
    offset = half_index % BLK
    positions = jnp.concatenate([half_index, (2 * N_CTX - 1 - block_index) * BLK + offset]).astype(jnp.int32)
    weights = tuple((matrix.astype(jnp.float32) for matrix in (norm_attn, w_query, key_projection, value_projection, w_out, norm_ffn, w_gate, w_up, w_down)))
    section_zero = tuple((matrix[0] for matrix in weights))
    section_one = tuple((matrix[1] for matrix in weights))

    def run_layer(values, params):
        return layer(values, positions, params)

    def one_sequence(running, item_pair):
        inputs, upstream = item_pair
        first_out, first_back = jax.vjp(run_layer, inputs.astype(jnp.float32), section_zero)
        passed = lower_precision(first_out)
        second_out, second_back = jax.vjp(run_layer, passed, section_one)
        grad_passed, grad_one = second_back(upstream.astype(jnp.float32))
        grad_passed = lower_precision(grad_passed)
        grad_inputs, grad_zero = first_back(grad_passed)
        running_zero, running_one = running
        running_zero = tuple((total + extra for total, extra in zip(running_zero, grad_zero)))
        running_one = tuple((total + extra for total, extra in zip(running_one, grad_one)))
        return ((running_zero, running_one), (passed.astype(jnp.bfloat16), second_out.astype(jnp.bfloat16), grad_inputs, grad_passed))
    sequences = tokens.reshape(MICRO * SEQS, LENGTH, MODEL_DIMENSION)
    upstreams = cotangent.reshape(MICRO * SEQS, LENGTH, MODEL_DIMENSION)
    start_sums = (tuple((jnp.zeros_like(matrix) for matrix in section_zero)), tuple((jnp.zeros_like(matrix) for matrix in section_one)))
    sums, (acts_zero, acts_one, grads_zero, grads_one) = lax.scan(one_sequence, start_sums, (sequences, upstreams))
    shape_out = (2, MICRO, SEQS, 2, LENGTH // 2, MODEL_DIMENSION)
    acts = jnp.stack([acts_zero, acts_one]).reshape(shape_out)
    in_grads = jnp.stack([grads_zero, grads_one]).reshape(shape_out)
    grads = tuple((jnp.stack([zero_part, one_part]) for zero_part, one_part in zip(sums[0], sums[1])))
    return (acts, in_grads, grads[0], grads[1], grads[2], grads[3], grads[4], grads[5], grads[6], grads[7], grads[8])
```

```python
import functools

import jax
import jax.numpy as jnp
from jax import lax
from jax.experimental import pallas as pl
from jax.experimental.pallas import tpu as pltpu
from jax.sharding import PartitionSpec as P

WIDTH = 960
HEADS = 15
KV_HEADS = 5
GROUP = HEADS // KV_HEADS
HEAD = 64
FF = 2560
BLK = 48
ROWS = 2 * BLK
CTX = 16
FSDP = 4
LENGTH = ROWS * CTX
SHARD = WIDTH // FSDP
FF_SHARD = FF // FSDP
QK_COLS = (HEADS + KV_HEADS) * HEAD
QKV_COLS = QK_COLS + KV_HEADS * HEAD
SLICE = 16
SLICES = SHARD // SLICE
DOWN_SLICE = FF_SHARD // CTX
TILE = 256

EPSILON = 1e-05
THETA = 10000.0
MASKED = -1e30

F32 = jnp.float32
BF16 = jnp.bfloat16


def sds(shape, dtype):
    return jax.ShapeDtypeStruct(shape, dtype)


def call(body, outs, *args, scratch=(), flops=0):
    size = sum(a.size * a.dtype.itemsize for a in (*args, *outs))
    return pl.pallas_call(
        body,
        out_shape=outs,
        scratch_shapes=list(scratch),
        compiler_params=pltpu.CompilerParams(vmem_limit_bytes=56 * 1024 * 1024),
        cost_estimate=pl.CostEstimate(flops=flops, bytes_accessed=size, transcendentals=0),
    )(*args)


def dot(a, b):
    return jnp.dot(a, b, preferred_element_type=F32)


def dot_t(a, b):
    return lax.dot_general(a, b, (((1,), (1,)), ((), ())), preferred_element_type=F32)


def t_dot(a, b):
    return lax.dot_general(a, b, (((0,), (0,)), ((), ())), preferred_element_type=F32)


def inverse_rms(x):
    return lax.rsqrt(jnp.mean(x * x, axis=-1, keepdims=True) + EPSILON)


def norm_backward(d, x, gain):
    r = inverse_rms(x)
    n = x * r
    t = d * gain
    return (t - n * jnp.mean(t * n, axis=-1, keepdims=True)) * r, jnp.sum(d * n, axis=0, keepdims=True)


def swap_halves(x):
    cols = x.shape[1]
    lane = lax.broadcasted_iota(jnp.int32, x.shape, 1)
    ahead = pltpu.roll(x, cols - HEAD // 2, 1)
    behind = pltpu.roll(x, HEAD // 2, 1)
    return jnp.where(lane % HEAD < HEAD // 2, ahead, behind)


def source_block(b):
    return (b, 0) if b < CTX else (2 * CTX - 1 - b, 1)


def qkv_body(count, *refs):
    parts, (gain, w, cos, sin) = refs[:count], refs[count : count + 4]
    x_out, a_out, send = refs[count + 4 :]
    x = parts[0][...].astype(F32)
    for part in parts[1:]:
        x = x + part[...].astype(F32)
    low = x.astype(BF16)
    x_out[...] = low
    x = low.astype(F32)
    a = x * inverse_rms(x) * gain[...]
    for k in range(FSDP):
        a_out[k] = a[:, k * SHARD : (k + 1) * SHARD].astype(BF16)
    out = dot(a.astype(BF16), w[...])
    qk = out[:, :QK_COLS]
    qk = qk * cos[...] + swap_halves(qk) * sin[...]
    v = out[:, QK_COLS:]
    for h in range(HEADS):
        g = h // GROUP
        q_h = qk[:, h * HEAD : (h + 1) * HEAD]
        k_g = qk[:, (HEADS + g) * HEAD : (HEADS + g + 1) * HEAD]
        v_g = v[:, g * HEAD : (g + 1) * HEAD]
        send[h, 0:ROWS] = jnp.concatenate([q_h, k_g], axis=1).astype(BF16)
        send[h, ROWS:] = jnp.concatenate([v_g[:BLK], v_g[BLK:]], axis=1).astype(BF16)
    for h in range(HEADS, CTX):
        send[h] = jnp.zeros(send.shape[1:], BF16)


def unpack_heads(recv, q_s, k_s, v_s):
    for b in range(2 * CTX):
        c, half = source_block(b)
        rows = slice(b * BLK, (b + 1) * BLK)
        qk = recv[c, half * BLK : (half + 1) * BLK, :].astype(F32)
        v = recv[c, ROWS : ROWS + BLK, :].astype(F32)
        q_s[rows, :] = qk[:, :HEAD].astype(BF16)
        k_s[rows, :] = qk[:, HEAD:].astype(BF16)
        v_s[rows, :] = v[:, half * HEAD : (half + 1) * HEAD].astype(BF16)


def probabilities(q, keys, start):
    scores = dot_t(q, keys)
    row = lax.broadcasted_iota(jnp.int32, scores.shape, 0) + start
    col = lax.broadcasted_iota(jnp.int32, scores.shape, 1)
    scores = jnp.where(col <= row, scores, MASKED)
    weights = jnp.exp(scores - jnp.max(scores, axis=-1, keepdims=True))
    return weights / jnp.sum(weights, axis=-1, keepdims=True)


def attend_body(recv, send, q_s, k_s, v_s, out_s):
    unpack_heads(recv, q_s, k_s, v_s)
    for i in range(LENGTH // TILE):
        start, stop = i * TILE, (i + 1) * TILE
        p = probabilities(q_s[start:stop, :], k_s[:stop, :], start)
        out_s[start:stop, :] = dot(p.astype(BF16), v_s[:stop, :])
    for c in range(CTX):
        last = 2 * CTX - 1 - c
        pair = [out_s[c * BLK : (c + 1) * BLK, :], out_s[last * BLK : (last + 1) * BLK, :]]
        send[c] = jnp.concatenate(pair, axis=1).astype(BF16)


def mix_body(x, recv, w_out, gain, mixed_out, b_out, att_out, att_s):
    for h in range(HEADS):
        pair = recv[h].astype(F32)
        cols = slice(h * HEAD, (h + 1) * HEAD)
        att_s[0:BLK, cols] = pair[:, :HEAD].astype(BF16)
        att_s[BLK:, cols] = pair[:, HEAD:].astype(BF16)
    att = att_s[...]
    for k in range(FSDP):
        att_out[k] = att_s[:, k * SHARD : (k + 1) * SHARD]
    mixed = x[...].astype(F32) + dot(att, w_out[...])
    mixed_out[...] = mixed
    b_out[...] = (mixed * inverse_rms(mixed) * gain[...]).astype(BF16)


def spread(total, outs):
    outs[0][...] = total[0:ROWS]
    for k in range(1, FSDP):
        outs[k][...] = total[k * ROWS : (k + 1) * ROWS].astype(BF16)


def ffn_body(*refs):
    parts, (w_gu, w_down), (gate_out, up_out), outs = refs[:4], refs[4:6], refs[6:8], refs[8:12]
    rows = jnp.concatenate([p[...] for p in parts], axis=0)
    gate = dot(rows, w_gu[:, :FF_SHARD])
    up = dot(rows, w_gu[:, FF_SHARD:])
    gate_out[...] = gate
    up_out[...] = up
    hidden = (gate * jax.nn.sigmoid(gate) * up).astype(BF16)
    spread(dot(hidden, w_down[...]), outs)


def ffn_back_body(*refs):
    parts, (gate_ref, up_ref, w_gu, w_down) = refs[:4], refs[4:8]
    hidden_out, d_gu_out = refs[8:10]
    outs = refs[10:14]
    rows = jnp.concatenate([p[...] for p in parts], axis=0)
    gate, up = gate_ref[...], up_ref[...]
    sig = jax.nn.sigmoid(gate)
    act = gate * sig
    hidden_out[...] = (act * up).astype(BF16)
    d_hidden = dot_t(rows, w_down[...])
    d_gate = (d_hidden * up * (sig * (1.0 + gate * (1.0 - sig)))).astype(BF16)
    d_up = (d_hidden * act).astype(BF16)
    d_gu_out[:, :FF_SHARD] = d_gate
    d_gu_out[:, FF_SHARD:] = d_up
    spread(dot_t(d_gate, w_gu[:, :FF_SHARD]) + dot_t(d_up, w_gu[:, FF_SHARD:]), outs)


def mix_back_body(g, p0, p1, p2, p3, mixed, gain, w_out, d_mixed_out, ga_out, gain_out, send):
    d_b = p0[...] + p1[...].astype(F32) + p2[...].astype(F32) + p3[...].astype(F32)
    d_in, d_gain = norm_backward(d_b, mixed[...], gain[...])
    d_mixed = g[...].astype(F32) + d_in
    d_mixed_out[...] = d_mixed
    gain_out[...] = d_gain
    ga = d_mixed.astype(BF16)
    ga_out[...] = ga
    d_att = dot_t(ga, w_out[...])
    for h in range(HEADS):
        piece = d_att[:, h * HEAD : (h + 1) * HEAD]
        send[h] = jnp.concatenate([piece[:BLK], piece[BLK:]], axis=1).astype(BF16)
    for h in range(HEADS, CTX):
        send[h] = jnp.zeros(send.shape[1:], BF16)


def attend_back_body(recv, d_recv, cos, sin, send, q_s, k_s, v_s, d_s, dq_s, dk_s, dv_s):
    unpack_heads(recv, q_s, k_s, v_s)
    for b in range(2 * CTX):
        c, half = source_block(b)
        pair = d_recv[c].astype(F32)
        d_s[b * BLK : (b + 1) * BLK, :] = pair[:, half * HEAD : (half + 1) * HEAD].astype(BF16)
    dk_s[...] = jnp.zeros(dk_s.shape, F32)
    dv_s[...] = jnp.zeros(dv_s.shape, F32)
    for i in range(LENGTH // TILE):
        start, stop = i * TILE, (i + 1) * TILE
        q, d_att = q_s[start:stop, :], d_s[start:stop, :]
        p = probabilities(q, k_s[:stop, :], start)
        d_p = dot_t(d_att, v_s[:stop, :])
        inner = jnp.sum(p * d_p, axis=-1, keepdims=True)
        d_scores = (p * (d_p - inner)).astype(BF16)
        dq_s[start:stop, :] = dot(d_scores, k_s[:stop, :])
        dk_s[:, :stop] += t_dot(q, d_scores)
        dv_s[:, :stop] += t_dot(d_att, p.astype(BF16))
    dk = dk_s[...].T
    dv = dv_s[...].T
    both = jnp.concatenate([dq_s[...] * (HEAD**-0.5), dk], axis=1)
    both = both * cos[...] + swap_halves(both) * sin[...]
    for c in range(CTX):
        last = 2 * CTX - 1 - c
        send[c, 0:BLK] = both[c * BLK : (c + 1) * BLK].astype(BF16)
        send[c, BLK:ROWS] = both[last * BLK : (last + 1) * BLK].astype(BF16)
        pair = [dv[c * BLK : (c + 1) * BLK], dv[last * BLK : (last + 1) * BLK]]
        send[c, ROWS:] = jnp.concatenate(pair, axis=1).astype(BF16)


def qkv_back_body(recv, d_mixed, x_ref, gain, w, gain_ffn, d_x_out, low_out, rows_out):
    for g in range(KV_HEADS):
        d_k = jnp.zeros((ROWS, HEAD), F32)
        d_v = jnp.zeros((BLK, 2 * HEAD), F32)
        for h in range(g * GROUP, (g + 1) * GROUP):
            qk = recv[h, 0:ROWS].astype(F32)
            rows_out[0:ROWS, h * HEAD : (h + 1) * HEAD] = qk[:, :HEAD].astype(BF16)
            d_k = d_k + qk[:, HEAD:]
            d_v = d_v + recv[h, ROWS:].astype(F32)
        k_cols = slice((HEADS + g) * HEAD, (HEADS + g + 1) * HEAD)
        v_cols = slice(QK_COLS + g * HEAD, QK_COLS + (g + 1) * HEAD)
        rows_out[0:ROWS, k_cols] = d_k.astype(BF16)
        rows_out[0:BLK, v_cols] = d_v[:, :HEAD].astype(BF16)
        rows_out[BLK:ROWS, v_cols] = d_v[:, HEAD:].astype(BF16)
    d_a = dot_t(rows_out[0:ROWS, :], w[...])
    d_in, d_gain = norm_backward(d_a, x_ref[...].astype(F32), gain[...])
    d_x = d_mixed[...] + d_in
    d_x_out[...] = d_x
    low_out[...] = d_x.astype(BF16)
    pad = jnp.zeros((6, WIDTH), F32)
    gains = jnp.concatenate([d_gain, gain_ffn[...], pad, jnp.zeros((8, WIDTH), F32)], axis=0)
    rows_out[ROWS:, :] = jnp.concatenate([gains, jnp.zeros((16, QKV_COLS - WIDTH), F32)], axis=1).astype(BF16)


def shifted(x, axis, distance):
    n = lax.axis_size(axis)
    return lax.ppermute(x, axis, [(i, (i + distance) % n) for i in range(n)])


def around(x):
    return [x] + [shifted(x, "fsdp", k) for k in range(1, FSDP)]


def back_around(parts):
    return [parts[0]] + [shifted(parts[k], "fsdp", -k) for k in range(1, FSDP)]


def exchange_blocks(blocks, index):
    pick = lambda k: lax.dynamic_index_in_dim(blocks, (index + k) % FSDP, 0, keepdims=False)
    return [pick(0)] + [shifted(pick(k), "fsdp", k) for k in range(1, FSDP)]


def swap_sections(x):
    return lax.ppermute(x, "section", [(0, 1), (1, 0)])


def all_to_all(x, axis):
    return lax.all_to_all(x, axis, 0, 0)


def on_device(
    tokens,
    cotangent,
    norm_attn,
    w_query,
    key_projection,
    value_projection,
    w_out,
    norm_ffn,
    w_gate,
    w_up,
    w_down,
):
    section = lax.axis_index("section")
    ctx = lax.axis_index("ctx")
    fsdp = lax.axis_index("fsdp")
    first = section == 0

    def my_slice(rows):
        padded = jnp.pad(rows, ((0, CTX * SLICE - SHARD), (0, 0)))
        return lax.dynamic_slice_in_dim(padded, ctx * SLICE, SLICE, 0)

    gains = jnp.stack([norm_attn[0], norm_ffn[0]])
    gains = lax.all_gather(gains, ("section", "fsdp")).reshape(2, FSDP, 2, SHARD)
    gains = gains.transpose(0, 2, 1, 3).reshape(2, 2, 1, WIDTH).astype(F32)

    qkv_slice = my_slice(jnp.concatenate([w_query[0], key_projection[0], value_projection[0]], axis=1))
    qkv_slices = all_to_all(
        jnp.broadcast_to(qkv_slice[None], (2 * FSDP, SLICE, QKV_COLS)), ("section", "fsdp")
    ).reshape(2, FSDP, SLICE, QKV_COLS)

    out_slice = my_slice(w_out[0])
    gate_slice = my_slice(w_gate[0]).reshape(SLICE, FSDP, FF_SHARD)
    up_slice = my_slice(w_up[0]).reshape(SLICE, FSDP, FF_SHARD)
    rest = jnp.concatenate(
        [jnp.broadcast_to(out_slice[:, None], (SLICE, FSDP, WIDTH)), gate_slice, up_slice], axis=2
    ).transpose(1, 0, 2)
    rest = jnp.broadcast_to(rest[None], (2,) + rest.shape).reshape((2 * FSDP,) + rest.shape[1:])
    rest_slices = all_to_all(rest, ("section", "fsdp")).reshape((2, FSDP) + rest.shape[1:])

    down_slice = lax.dynamic_slice_in_dim(w_down[0], ctx * DOWN_SLICE, DOWN_SLICE, 0)
    down_other = swap_sections(down_slice)
    down_slices = (jnp.where(first, down_slice, down_other), jnp.where(first, down_other, down_slice))

    def whole(slices):
        gathered = lax.all_gather(slices, "ctx")[:SLICES]
        return gathered.transpose(1, 0, 2, 3).reshape(WIDTH, slices.shape[-1])

    qkv_weights, out_weights, gu_weights, down_weights = [], [], [], []
    for layer in range(2):
        qkv_weights.append(whole(qkv_slices[layer]))
        both = whole(rest_slices[layer])
        out_weights.append(both[:, :WIDTH])
        gu_weights.append(both[:, WIDTH:])
        down_weights.append(lax.all_gather(down_slices[layer], "ctx", tiled=True))

    inverse = THETA ** (-(jnp.arange(HEAD // 2, dtype=F32) * 2.0) / HEAD)

    def tables(positions):
        angles = positions.astype(F32)[:, None] * inverse[None, :]
        return jnp.cos(angles), jnp.sin(angles)

    offset = jnp.arange(BLK, dtype=jnp.int32)
    own = jnp.concatenate([ctx * BLK + offset, (2 * CTX - 1 - ctx) * BLK + offset])
    cos, sin = tables(own)
    scale = jnp.where(jnp.arange(QK_COLS) < HEADS * HEAD, HEAD**-0.5, 1.0)[None, :]
    cos_own = jnp.tile(jnp.concatenate([cos, cos], axis=1), (1, HEADS + KV_HEADS)) * scale
    sin_own = jnp.tile(jnp.concatenate([-sin, sin], axis=1), (1, HEADS + KV_HEADS)) * scale
    cos, sin = tables(jnp.arange(LENGTH, dtype=jnp.int32))
    cos_all = jnp.concatenate([cos, cos] * 2, axis=1)
    sin_all = jnp.concatenate([sin, -sin] * 2, axis=1)

    my_rows = lax.dynamic_index_in_dim(tokens, section, 0).reshape(ROWS, WIDTH)
    my_cotangent = lax.dynamic_index_in_dim(cotangent, section, 0).reshape(ROWS, WIDTH)

    row_f32, row_bf16 = sds((ROWS, WIDTH), F32), sds((ROWS, WIDTH), BF16)
    heads_shape = sds((CTX, ROWS + BLK, 2 * HEAD), BF16)
    att_shape = sds((CTX, BLK, 2 * HEAD), BF16)
    blocks_shape = sds((FSDP, ROWS, SHARD), BF16)
    seq = lambda dtype: pltpu.VMEM((LENGTH, HEAD), dtype)
    partials = [row_f32] + [row_bf16] * 3
    ff_f32, ff_bf16 = sds((FSDP * ROWS, FF_SHARD), F32), sds((FSDP * ROWS, FF_SHARD), BF16)

    kept = []
    parts = [my_rows]
    for layer in range(2):
        gain_attn, gain_ffn = gains[layer]
        x, a_blocks, send = call(
            functools.partial(qkv_body, len(parts)),
            [row_bf16, blocks_shape, heads_shape],
            *parts, gain_attn, qkv_weights[layer], cos_own, sin_own,
            flops=2 * ROWS * WIDTH * QKV_COLS,
        )
        heads = all_to_all(send, "ctx")
        send = call(
            attend_body, [att_shape], heads,
            scratch=[seq(BF16), seq(BF16), seq(BF16), seq(F32)],
            flops=2 * LENGTH * LENGTH * HEAD,
        )[0]
        mixed, b, att_blocks = call(
            mix_body, [row_f32, row_bf16, blocks_shape],
            x, all_to_all(send, "ctx"), out_weights[layer], gain_ffn,
            scratch=[pltpu.VMEM((ROWS, WIDTH), BF16)],
            flops=2 * ROWS * WIDTH * WIDTH,
        )
        b_all = around(b)
        gate, up, *outs = call(
            ffn_body, [ff_f32, ff_f32] + partials,
            *b_all, gu_weights[layer], down_weights[layer],
            flops=2 * FSDP * ROWS * WIDTH * FF_SHARD * 3,
        )
        parts = [mixed] + back_around(outs)
        kept.append((x, a_blocks, heads, mixed, att_blocks, b_all, gate, up))
    last = parts[0]
    for part in parts[1:]:
        last = last + part.astype(F32)
    first_acts, last_acts = kept[1][0], last.astype(BF16)

    g, g_low = my_cotangent, my_cotangent
    grads = [None, None]
    d_inputs = [None, None]
    for layer in (1, 0):
        gain_attn, gain_ffn = gains[layer]
        x, a_blocks, heads, mixed, att_blocks, b_all, gate, up = kept[layer]
        g_all = around(g_low)
        hidden, d_gu, *outs = call(
            ffn_back_body, [ff_bf16, sds((FSDP * ROWS, 2 * FF_SHARD), BF16)] + partials,
            *g_all, gate, up, gu_weights[layer], down_weights[layer],
            flops=2 * FSDP * ROWS * WIDTH * FF_SHARD * 3,
        )
        d_mixed, ga, d_gain_ffn, send = call(
            mix_back_body, [row_f32, row_bf16, sds((1, WIDTH), F32), att_shape],
            g, *back_around(outs), mixed, gain_ffn, out_weights[layer],
            flops=2 * ROWS * WIDTH * WIDTH,
        )
        send = call(
            attend_back_body, [heads_shape],
            heads, all_to_all(send, "ctx"), cos_all, sin_all,
            scratch=[seq(BF16)] * 4 + [seq(F32)] + [pltpu.VMEM((HEAD, LENGTH), F32)] * 2,
            flops=5 * LENGTH * LENGTH * HEAD,
        )[0]
        d_x, d_low, d_rows = call(
            qkv_back_body, [row_f32, row_bf16, sds((ROWS + 16, QKV_COLS), BF16)],
            all_to_all(send, "ctx"), d_mixed, x, gain_attn, qkv_weights[layer], d_gain_ffn,
            flops=2 * ROWS * WIDTH * QKV_COLS,
        )

        grad_gu = t_dot(jnp.concatenate(b_all), d_gu).astype(BF16)
        grad_down = t_dot(hidden, jnp.concatenate(g_all)).astype(BF16)
        grad_gu = grad_gu.reshape(FSDP, SLICES, SLICE, 2 * FF_SHARD).transpose(1, 0, 2, 3)
        grad_gu = jnp.pad(grad_gu, ((0, CTX - SLICES), (0, 0), (0, 0), (0, 0)))
        grad_gu = lax.psum_scatter(
            grad_gu.reshape(CTX * FSDP * SLICE, 2 * FF_SHARD), "ctx", scatter_dimension=0, tiled=True
        ).reshape(FSDP, SLICE, 2 * FF_SHARD)
        gu_slices = jnp.stack(exchange_blocks(grad_gu, fsdp))
        grad_down = lax.psum_scatter(grad_down, "ctx", scatter_dimension=0, tiled=True)

        a_cols = jnp.concatenate(exchange_blocks(a_blocks, fsdp))
        att_cols = jnp.concatenate(exchange_blocks(att_blocks, fsdp))
        ga_all = jnp.concatenate(around(ga))
        rows_all = jnp.stack(around(d_rows))
        grad_qkv = t_dot(a_cols, rows_all[:, :ROWS].reshape(FSDP * ROWS, QKV_COLS))
        grad_out = t_dot(att_cols, ga_all)
        gain_rows = rows_all[:, ROWS : ROWS + 2, :WIDTH].astype(F32).sum(axis=0)
        gain_rows = lax.dynamic_slice_in_dim(gain_rows, fsdp * SHARD, SHARD, 1)
        gain_rows = jnp.pad(gain_rows, ((0, SLICE - 2), (0, QKV_COLS - SHARD)))
        grad_qkv = jnp.concatenate([grad_qkv, gain_rows]).astype(BF16)
        grad_out = jnp.pad(grad_out, ((0, SLICE), (0, 0))).astype(BF16)

        def scatter(rows):
            arrived = all_to_all(rows.reshape(CTX, SLICE, rows.shape[1]), "ctx")
            return arrived.astype(F32).sum(axis=0).astype(BF16)

        grads[layer] = (gu_slices, grad_down, scatter(grad_out), scatter(grad_qkv))
        d_inputs[layer] = (d_x, d_low)
        g, g_low = d_low, d_low

    def across(zero, one):
        keep, give = jnp.where(first, zero, one), jnp.where(first, one, zero)
        return (keep.astype(F32) + swap_sections(give).astype(F32)).astype(BF16)

    gu_slices, down_slice, out_slice, qkv_slice = [across(zero, one) for zero, one in zip(*grads)]
    gu = lax.all_gather(gu_slices, "ctx")[:SLICES]
    down = lax.all_gather(down_slice, "ctx", tiled=True).astype(F32)
    out = lax.all_gather(out_slice, "ctx", tiled=True)[:SHARD].astype(F32)
    qkv = lax.all_gather(qkv_slice, "ctx", tiled=True)
    order = (fsdp - jnp.arange(FSDP)) % FSDP
    gu = gu[:, order].transpose(0, 2, 1, 3).reshape(SHARD, FSDP, 2, FF_SHARD).astype(F32)
    gate_grad = gu[:, :, 0].reshape(SHARD, FF)
    up_grad = gu[:, :, 1].reshape(SHARD, FF)
    gain_rows = qkv[SHARD : SHARD + 2, :SHARD].astype(F32)
    qkv = qkv[:SHARD].astype(F32)

    other_acts = swap_sections(jnp.where(first, last_acts, first_acts))
    mine_acts = jnp.where(first, first_acts, last_acts)
    d_zero, d_one = d_inputs[0][0], d_inputs[1][1].astype(F32)
    other_grads = swap_sections(jnp.where(first, d_one, d_zero))
    mine_grads = jnp.where(first, d_zero, d_one)

    def by_micro(mine, other):
        pair = jnp.stack([jnp.where(first, mine, other), jnp.where(first, other, mine)])
        return pair.reshape(1, 2, 1, 2, BLK, WIDTH)

    kv = KV_HEADS * HEAD
    return (
        by_micro(mine_acts, other_acts),
        by_micro(mine_grads, other_grads),
        gain_rows[0:1],
        qkv[None, :, :WIDTH],
        qkv[None, :, WIDTH : WIDTH + kv],
        qkv[None, :, WIDTH + kv :],
        out[None],
        gain_rows[1:2],
        gate_grad[None],
        up_grad[None],
        down[None],
    )


def solution(mesh):
    rows = P(None, "fsdp", None, "ctx", None)
    gain, matrix = P("section", "fsdp"), P("section", "fsdp", None)
    layer_rows = P("section", None, "fsdp", None, "ctx", None)
    weights = (gain, matrix, matrix, matrix, matrix, gain, matrix, matrix, matrix)
    return jax.shard_map(
        on_device,
        mesh=mesh,
        in_specs=(rows, rows) + weights,
        out_specs=(layer_rows, layer_rows) + weights,
        check_vma=False,
    )
```

```python
import functools

import jax
import jax.numpy as jnp
import numpy as np
from jax import lax
from jax.experimental import pallas as pl
from jax.experimental.pallas import tpu as pltpu
from jax.sharding import PartitionSpec as P

WIDTH = 960
HEADS = 15
KV_HEADS = 5
GROUP = HEADS // KV_HEADS
HEAD = 64
FF = 2560
BLK = 48
ROWS = 2 * BLK
CTX = 16
FSDP = 4
LENGTH = ROWS * CTX
SHARD = WIDTH // FSDP
FF_SHARD = FF // FSDP
QK_COLS = (HEADS + KV_HEADS) * HEAD
QKV_COLS = QK_COLS + KV_HEADS * HEAD
SLICE = 16
SLICES = SHARD // SLICE
DOWN_SLICE = WIDTH // SLICES
OUT_COLS = QKV_COLS + WIDTH
FFN_COLS = 3 * FF_SHARD
QKV_LANES = 1664
OUT_LANES = 1024
TILE = 256

EPSILON = 1e-05
THETA = 10000.0
MASKED = -1e30

F32 = jnp.float32
BF16 = jnp.bfloat16


def sds(shape, dtype):
    return jax.ShapeDtypeStruct(shape, dtype)


def call(body, outs, *args, far=(), scalars=0, scratch=(), flops=0):
    size = sum(a.size * a.dtype.itemsize for a in (*args, *outs))
    specs = [pl.BlockSpec(memory_space=pltpu.SMEM if i < scalars else pltpu.VMEM) for i in range(len(args))]
    return pl.pallas_call(
        body,
        out_shape=outs,
        in_specs=specs + [pl.BlockSpec(memory_space=pl.ANY)] * len(far),
        scratch_shapes=list(scratch),
        compiler_params=pltpu.CompilerParams(vmem_limit_bytes=56 * 1024 * 1024),
        cost_estimate=pl.CostEstimate(flops=flops, bytes_accessed=size, transcendentals=0),
    )(*args, *far)


def dot(a, b):
    return jnp.dot(a, b, preferred_element_type=F32)


def dot_t(a, b):
    return lax.dot_general(a, b, (((1,), (1,)), ((), ())), preferred_element_type=F32)


def t_dot(a, b):
    return lax.dot_general(a, b, (((0,), (0,)), ((), ())), preferred_element_type=F32)


def inverse_rms(x):
    return lax.rsqrt(jnp.mean(x * x, axis=-1, keepdims=True) + EPSILON)


def norm_backward(d, x, gain):
    r = inverse_rms(x)
    n = x * r
    t = d * gain
    return (t - n * jnp.mean(t * n, axis=-1, keepdims=True)) * r, jnp.sum(d * n, axis=0, keepdims=True)


def swap_halves(x):
    cols = x.shape[1]
    lane = lax.broadcasted_iota(jnp.int32, x.shape, 1)
    ahead = pltpu.roll(x, cols - HEAD // 2, 1)
    behind = pltpu.roll(x, HEAD // 2, 1)
    return jnp.where(lane % HEAD < HEAD // 2, ahead, behind)


def source_block(b):
    return (b, 0) if b < CTX else (2 * CTX - 1 - b, 1)


def rotary_constants():
    inverse = (THETA ** (-(np.arange(HEAD // 2, dtype=np.float32) * 2.0) / HEAD)).astype(np.float32)
    angles = np.arange(LENGTH, dtype=np.float32)[:, None] * inverse[None, :]
    cos, sin = np.cos(angles.astype(np.float64)), np.sin(angles.astype(np.float64))
    return (
        np.concatenate([cos] * 4, axis=1).astype(np.float32),
        np.concatenate([-sin, sin] * 2, axis=1).astype(np.float32),
    )


def pack(x):
    return jnp.concatenate([x[:BLK], x[BLK:]], axis=1)


def unpack(x):
    cols = x.shape[1] // 2
    return jnp.concatenate([x[:, :cols], x[:, cols:]], axis=0)


def load_rows(src, lanes, dst, sems):
    copies = [
        pltpu.make_async_copy(src.at[0:SLICES, f * SLICE : (f + 1) * SLICE, lanes], dst.at[f], sems.at[f])
        for f in range(FSDP)
    ]
    for copy in copies:
        copy.start()
    return copies


def load_down(src, lanes, dst, sem):
    copy = pltpu.make_async_copy(src.at[0:SLICES, :, lanes], dst, sem)
    copy.start()
    return [copy]


def wait_all(copies):
    for copy in copies:
        copy.wait()


def rows_of(scratch):
    return scratch[...].reshape(WIDTH, scratch.shape[-1])


def row_scratch(lanes):
    return [pltpu.VMEM((FSDP, SLICES, SLICE, lanes), BF16), pltpu.SemaphoreType.DMA((FSDP,))]


def qkv_body(count, *refs):
    parts, (gain, cos, sin, w_far) = refs[:count], refs[count : count + 4]
    x_out, a_out, send, w_s, sems = refs[count + 4 :]
    copies = load_rows(w_far, slice(0, QKV_LANES), w_s, sems)
    x = parts[0][...].astype(F32)
    if count > 1:
        x = x + parts[1][...]
        for part in parts[2:]:
            x = x + unpack(part[...].astype(F32))
    low = x.astype(BF16)
    x_out[...] = low
    x = low.astype(F32)
    a = x * inverse_rms(x) * gain[...]
    for k in range(FSDP):
        a_out[k] = a[:, k * SHARD : (k + 1) * SHARD].astype(BF16)
    wait_all(copies)
    out = dot(a.astype(BF16), rows_of(w_s))
    qk = out[:, :QK_COLS]
    pairs = (HEADS + KV_HEADS) // 2
    lane = lax.broadcasted_iota(jnp.int32, qk.shape, 1)
    scale = jnp.where(lane < HEADS * HEAD, HEAD**-0.5, 1.0)
    cos_all = jnp.concatenate([cos[...]] * pairs, axis=1) * scale
    sin_all = jnp.concatenate([sin[...]] * pairs, axis=1) * scale
    qk = qk * cos_all + swap_halves(qk) * sin_all
    v = out[:, QK_COLS:QKV_COLS]
    for h in range(HEADS):
        g = h // GROUP
        q_h = qk[:, h * HEAD : (h + 1) * HEAD]
        k_g = qk[:, (HEADS + g) * HEAD : (HEADS + g + 1) * HEAD]
        v_g = v[:, g * HEAD : (g + 1) * HEAD]
        send[h, 0:ROWS] = jnp.concatenate([q_h, k_g], axis=1).astype(BF16)
        send[h, ROWS:] = pack(v_g).astype(BF16)
    for h in range(HEADS, CTX):
        send[h] = jnp.zeros(send.shape[1:], BF16)


def unpack_heads(recv, q_s, k_s, v_s):
    for b in range(2 * CTX):
        c, half = source_block(b)
        rows = slice(b * BLK, (b + 1) * BLK)
        qk = recv[c, half * BLK : (half + 1) * BLK, :].astype(F32)
        v = recv[c, ROWS : ROWS + BLK, :].astype(F32)
        q_s[rows, :] = qk[:, :HEAD].astype(BF16)
        k_s[rows, :] = qk[:, HEAD:].astype(BF16)
        v_s[rows, :] = v[:, half * HEAD : (half + 1) * HEAD].astype(BF16)


def probabilities(q, keys, start):
    scores = dot_t(q, keys)
    row = lax.broadcasted_iota(jnp.int32, scores.shape, 0) + start
    col = lax.broadcasted_iota(jnp.int32, scores.shape, 1)
    scores = jnp.where(col <= row, scores, MASKED)
    weights = jnp.exp(scores - jnp.max(scores, axis=-1, keepdims=True))
    return weights / jnp.sum(weights, axis=-1, keepdims=True)


def attend_body(recv, send, q_s, k_s, v_s, out_s):
    unpack_heads(recv, q_s, k_s, v_s)
    for i in range(LENGTH // TILE):
        start, stop = i * TILE, (i + 1) * TILE
        p = probabilities(q_s[start:stop, :], k_s[:stop, :], start)
        out_s[start:stop, :] = dot(p.astype(BF16), v_s[:stop, :])
    for c in range(CTX):
        last = 2 * CTX - 1 - c
        pair = [out_s[c * BLK : (c + 1) * BLK, :], out_s[last * BLK : (last + 1) * BLK, :]]
        send[c] = jnp.concatenate(pair, axis=1).astype(BF16)


def mix_body(x, recv, gain, w_far, mixed_out, b_out, att_out, att_s, w_s, sems):
    copies = load_rows(w_far, slice(0, OUT_LANES), w_s, sems)
    for h in range(HEADS):
        pair = recv[h].astype(F32)
        cols = slice(h * HEAD, (h + 1) * HEAD)
        att_s[0:BLK, cols] = pair[:, :HEAD].astype(BF16)
        att_s[BLK:, cols] = pair[:, HEAD:].astype(BF16)
    att = att_s[...]
    for k in range(FSDP):
        att_out[k] = att_s[:, k * SHARD : (k + 1) * SHARD]
    wait_all(copies)
    mixed = x[...].astype(F32) + dot(att, rows_of(w_s))[:, :WIDTH]
    mixed_out[...] = mixed
    b_out[...] = pack(mixed * inverse_rms(mixed) * gain[...]).astype(BF16)


def spread(total, outs):
    outs[0][...] = total[0:ROWS]
    for k in range(1, FSDP):
        outs[k][...] = pack(total[k * ROWS : (k + 1) * ROWS]).astype(BF16)


def all_rows(parts):
    return jnp.concatenate([unpack(p[...]) for p in parts], axis=0)


def ffn_body(*refs):
    parts, w_far, (gate_out, up_out), outs = refs[:4], refs[4], refs[5:7], refs[7:11]
    w_s, sems, down_s, down_sem = refs[11:]
    copies = load_rows(w_far, slice(OUT_LANES, OUT_LANES + 2 * FF_SHARD), w_s, sems)
    down = load_down(w_far, slice(OUT_LANES + 2 * FF_SHARD, OUT_LANES + FFN_COLS), down_s, down_sem)
    rows = all_rows(parts)
    wait_all(copies)
    gate_up = dot(rows, rows_of(w_s))
    gate, up = gate_up[:, :FF_SHARD], gate_up[:, FF_SHARD:]
    gate_out[...] = gate
    up_out[...] = up
    hidden = (gate * jax.nn.sigmoid(gate) * up).astype(BF16)
    wait_all(down)
    spread(dot_t(hidden, rows_of(down_s)), outs)


def ffn_back_body(*refs):
    parts, (gate_ref, up_ref, w_far) = refs[:4], refs[4:7]
    hidden_out, d_gu_out = refs[7:9]
    outs = refs[9:13]
    w_s, sems, down_s, down_sem = refs[13:]
    down = load_down(w_far, slice(OUT_LANES + 2 * FF_SHARD, OUT_LANES + FFN_COLS), down_s, down_sem)
    copies = load_rows(w_far, slice(OUT_LANES, OUT_LANES + 2 * FF_SHARD), w_s, sems)
    rows = all_rows(parts)
    gate, up = gate_ref[...], up_ref[...]
    sig = jax.nn.sigmoid(gate)
    act = gate * sig
    hidden_out[...] = (act * up).astype(BF16)
    wait_all(down)
    d_hidden = dot(rows, rows_of(down_s))
    d_gu_out[:, :FF_SHARD] = (d_hidden * up * (sig * (1.0 + gate * (1.0 - sig)))).astype(BF16)
    d_gu_out[:, FF_SHARD:] = (d_hidden * act).astype(BF16)
    wait_all(copies)
    spread(dot_t(d_gu_out[...], rows_of(w_s)), outs)


def ffn_grad_body(*refs):
    b_parts, g_parts, d_gu, hidden, out = refs[:4], refs[4:8], refs[8], refs[9], refs[10]
    gu = t_dot(all_rows(b_parts), d_gu[...]).astype(BF16)
    for f in range(FSDP):
        for c in range(SLICES):
            first = f * SHARD + c * SLICE
            out[c, f * SLICE : (f + 1) * SLICE, 0 : 2 * FF_SHARD] = gu[first : first + SLICE]
    down = t_dot(all_rows(g_parts), hidden[...]).astype(BF16)
    for c in range(SLICES):
        out[c, :, 2 * FF_SHARD :] = down[c * DOWN_SLICE : (c + 1) * DOWN_SLICE]
    for c in range(SLICES, CTX):
        out[c] = jnp.zeros(out.shape[1:], BF16)


def mix_back_body(g, p0, p1, p2, p3, mixed, gain, w_far, d_mixed_out, ga_out, gain_out, send, w_s, sems):
    copies = load_rows(w_far, slice(0, OUT_LANES), w_s, sems)
    d_b = p0[...]
    for part in (p1, p2, p3):
        d_b = d_b + unpack(part[...].astype(F32))
    d_in, d_gain = norm_backward(d_b, mixed[...], gain[...])
    d_mixed = unpack(g[...].astype(F32)) + d_in
    d_mixed_out[...] = d_mixed
    gain_out[...] = d_gain
    ga_out[...] = pack(d_mixed).astype(BF16)
    wide = jnp.concatenate([d_mixed, jnp.zeros((ROWS, OUT_LANES - WIDTH), F32)], axis=1).astype(BF16)
    wait_all(copies)
    d_att = dot_t(wide, rows_of(w_s))
    for h in range(HEADS):
        send[h] = pack(d_att[:, h * HEAD : (h + 1) * HEAD]).astype(BF16)
    for h in range(HEADS, CTX):
        send[h] = jnp.zeros(send.shape[1:], BF16)


def attend_back_body(recv, d_recv, cos, sin, send, q_s, k_s, v_s, d_s, dq_s, dk_s, dv_s):
    unpack_heads(recv, q_s, k_s, v_s)
    for b in range(2 * CTX):
        c, half = source_block(b)
        pair = d_recv[c].astype(F32)
        d_s[b * BLK : (b + 1) * BLK, :] = pair[:, half * HEAD : (half + 1) * HEAD].astype(BF16)
    dk_s[...] = jnp.zeros(dk_s.shape, F32)
    dv_s[...] = jnp.zeros(dv_s.shape, F32)
    for i in range(LENGTH // TILE):
        start, stop = i * TILE, (i + 1) * TILE
        q, d_att = q_s[start:stop, :], d_s[start:stop, :]
        p = probabilities(q, k_s[:stop, :], start)
        d_p = dot_t(d_att, v_s[:stop, :])
        inner = jnp.sum(p * d_p, axis=-1, keepdims=True)
        d_scores = (p * (d_p - inner)).astype(BF16)
        dq_s[start:stop, :] = dot(d_scores, k_s[:stop, :])
        dk_s[:, :stop] += t_dot(q, d_scores)
        dv_s[:, :stop] += t_dot(d_att, p.astype(BF16))
    dk = dk_s[...].T
    dv = dv_s[...].T
    both = jnp.concatenate([dq_s[...] * (HEAD**-0.5), dk], axis=1)
    both = both * cos[...] - swap_halves(both) * sin[...]
    for c in range(CTX):
        last = 2 * CTX - 1 - c
        send[c, 0:BLK] = both[c * BLK : (c + 1) * BLK].astype(BF16)
        send[c, BLK:ROWS] = both[last * BLK : (last + 1) * BLK].astype(BF16)
        pair = [dv[c * BLK : (c + 1) * BLK], dv[last * BLK : (last + 1) * BLK]]
        send[c, ROWS:] = jnp.concatenate(pair, axis=1).astype(BF16)


def qkv_back_body(recv, d_mixed, x_ref, gain, gain_ffn, w_far, d_x_out, low_out, rows_out, rows_s, w_s, sems):
    copies = load_rows(w_far, slice(0, QKV_LANES), w_s, sems)
    rows_s[:, QKV_COLS:] = jnp.zeros((ROWS, QKV_LANES - QKV_COLS), BF16)
    for g in range(KV_HEADS):
        d_k = jnp.zeros((ROWS, HEAD), F32)
        d_v = jnp.zeros((BLK, 2 * HEAD), F32)
        for h in range(g * GROUP, (g + 1) * GROUP):
            qk = recv[h, 0:ROWS].astype(F32)
            rows_s[:, h * HEAD : (h + 1) * HEAD] = qk[:, :HEAD].astype(BF16)
            d_k = d_k + qk[:, HEAD:]
            d_v = d_v + recv[h, ROWS:].astype(F32)
        k_cols = slice((HEADS + g) * HEAD, (HEADS + g + 1) * HEAD)
        v_cols = slice(QK_COLS + g * HEAD, QK_COLS + (g + 1) * HEAD)
        rows_s[:, k_cols] = d_k.astype(BF16)
        rows_s[:, v_cols] = unpack(d_v).astype(BF16)
    rows = rows_s[...]
    rows_out[0:ROWS] = rows
    wait_all(copies)
    d_a = dot_t(rows, rows_of(w_s))
    d_in, d_gain = norm_backward(d_a, x_ref[...].astype(F32), gain[...])
    d_x = d_mixed[...] + d_in
    d_x_out[...] = d_x
    low_out[...] = pack(d_x).astype(BF16)
    gains = jnp.concatenate([d_gain, gain_ffn[...], jnp.zeros((SLICE - 2, WIDTH), F32)], axis=0)
    gains = jnp.concatenate([gains, jnp.zeros((SLICE, QKV_LANES - WIDTH), F32)], axis=1)
    rows_out[ROWS:] = gains.astype(BF16)


def qkv_grad_body(fsdp_ref, *refs):
    blocks, parts, out = refs[:4], refs[4:8], refs[8]
    cols = jnp.concatenate([p[:, :SHARD] for p in blocks], axis=0)
    rows = jnp.concatenate([p[0:ROWS] for p in parts], axis=0)
    grad = t_dot(cols, rows).astype(BF16)
    for c in range(SLICES):
        out[c] = grad[c * SLICE : (c + 1) * SLICE]
    gains = sum(p[ROWS:].astype(F32) for p in parts)
    mine = jnp.zeros((SLICE, SHARD), F32)
    for f in range(FSDP):
        mine = jnp.where(fsdp_ref[0] == f, gains[:, f * SHARD : (f + 1) * SHARD], mine)
    out[SLICES] = jnp.concatenate([mine, jnp.zeros((SLICE, QKV_LANES - SHARD), F32)], axis=1).astype(BF16)


def out_grad_body(*refs):
    blocks, ga_parts, out = refs[:4], refs[4:8], refs[8]
    cols = jnp.concatenate([p[:, SHARD:] for p in blocks], axis=0)
    grad = t_dot(cols, all_rows(ga_parts))
    grad = jnp.concatenate([grad, jnp.zeros((SHARD, OUT_LANES - WIDTH), F32)], axis=1).astype(BF16)
    for c in range(SLICES):
        out[c] = grad[c * SLICE : (c + 1) * SLICE]
    out[SLICES] = jnp.zeros((SLICE, OUT_LANES), BF16)


def rest_result_body(fsdp_ref, gathered, gate, up, down, out):
    for c in range(SLICES):
        rows = slice(c * SLICE, (c + 1) * SLICE)
        for k in range(FSDP):
            member = lax.rem(fsdp_ref[0] + FSDP - k, FSDP)
            cols = pl.ds(pl.multiple_of(member * FF_SHARD, 128), FF_SHARD)
            piece = gathered[c, k * SLICE : (k + 1) * SLICE, : 2 * FF_SHARD].astype(F32)
            gate[rows, cols] = piece[:, :FF_SHARD]
            up[rows, cols] = piece[:, FF_SHARD:]
        down[c * DOWN_SLICE : (c + 1) * DOWN_SLICE] = gathered[c, 0 : FSDP * SLICE, 2 * FF_SHARD : FFN_COLS].astype(F32)
        out[rows] = gathered[c, FSDP * SLICE :, :WIDTH].astype(F32)


def qkv_result_body(gathered, query, key, value, gains, kv_s):
    kv = KV_HEADS * HEAD
    for c in range(SLICES):
        rows = slice(c * SLICE, (c + 1) * SLICE)
        piece = gathered[c].astype(F32)
        query[rows] = piece[:, :WIDTH]
        kv_s[rows] = piece[:, WIDTH:QKV_COLS]
    turned = kv_s[...].T
    key[...] = turned[:kv]
    value[...] = turned[kv:]
    gains[...] = gathered[SLICES][:8, :SHARD].astype(F32)


def shifted(x, axis, distance):
    n = lax.axis_size(axis)
    return lax.ppermute(x, axis, [(i, (i + distance) % n) for i in range(n)])


def around(x):
    return [x] + [shifted(x, "fsdp", k) for k in range(1, FSDP)]


def back_around(parts):
    return [parts[0]] + [shifted(parts[k], "fsdp", -k) for k in range(1, FSDP)]


def exchange_blocks(blocks, index):
    pick = lambda k: lax.dynamic_index_in_dim(blocks, (index + k) % FSDP, 0, keepdims=False)
    return [pick(0)] + [shifted(pick(k), "fsdp", k) for k in range(1, FSDP)]


def swap_sections(x):
    return lax.ppermute(x, "section", [(0, 1), (1, 0)])


def all_to_all(x, axis):
    return lax.all_to_all(x, axis, 0, 0)


def after(x, *earlier):
    return lax.optimization_barrier((x, earlier))[0]


def to_all(x, axis, count):
    return all_to_all(jnp.broadcast_to(x[None], (count,) + x.shape), axis)


def on_device(
    tokens,
    cotangent,
    norm_attn,
    w_query,
    key_projection,
    value_projection,
    w_out,
    norm_ffn,
    w_gate,
    w_up,
    w_down,
):
    section = lax.axis_index("section")
    ctx = lax.axis_index("ctx")
    fsdp = lax.axis_index("fsdp")
    first = section == 0

    place = jnp.minimum(ctx, SLICES - 1)

    def my_slice(rows, count=SLICE):
        return lax.dynamic_slice_in_dim(rows, place * count, count, 0)

    own_gains = jnp.concatenate([norm_attn, norm_ffn], axis=1)
    own_gains = jnp.pad(own_gains, ((0, SLICE - 1), (0, QKV_LANES - 2 * SHARD)))
    qkv = jnp.concatenate([my_slice(w[0]) for w in (w_query, key_projection, value_projection)], axis=1)
    qkv = jnp.pad(qkv, ((0, 0), (0, QKV_LANES - QKV_COLS)))
    qkv = to_all(jnp.where(ctx < SLICES, qkv, own_gains), ("section", "fsdp"), 2 * FSDP)
    qkv = qkv.reshape(2, FSDP * SLICE, QKV_LANES)

    out = jnp.pad(my_slice(w_out[0]), ((0, 0), (0, OUT_LANES - WIDTH)))
    out = jnp.broadcast_to(out[:, None], (SLICE, FSDP, OUT_LANES))
    rest = [my_slice(w[0]).reshape(SLICE, FSDP, FF_SHARD) for w in (w_gate, w_up)]
    rest = jnp.concatenate([out] + rest, axis=2).transpose(1, 0, 2)
    rest = all_to_all(after(jnp.concatenate([rest, rest]), qkv), ("section", "fsdp"))
    rest = rest.reshape(2, FSDP * SLICE, OUT_LANES + 2 * FF_SHARD)
    down = my_slice(w_down[0].T, DOWN_SLICE)
    down_other = swap_sections(after(down, qkv))
    downs = (jnp.where(first, down, down_other), jnp.where(first, down_other, down))
    rest = [jnp.concatenate(pair, axis=1) for pair in zip(rest, downs)]

    qkv_weights, rest_weights = [lax.all_gather(qkv[0], "ctx")], []

    def gains_of(layer):
        rows = qkv_weights[layer][SLICES, ::SLICE, : 2 * SHARD].astype(F32)
        return rows[:, :SHARD].reshape(1, WIDTH), rows[:, SHARD:].reshape(1, WIDTH)

    cos_all, sin_all = rotary_constants()
    cos_all, sin_all = jnp.asarray(cos_all), jnp.asarray(sin_all)

    def own_positions(table):
        pieces = [
            lax.dynamic_slice_in_dim(table, start * BLK, BLK, 0) for start in (ctx, 2 * CTX - 1 - ctx)
        ]
        return jnp.concatenate(pieces)

    cos_own, sin_own = own_positions(cos_all), own_positions(sin_all)

    def mine(x):
        return lax.dynamic_index_in_dim(x, section, 0, keepdims=False).reshape(2, BLK, WIDTH)

    my_rows = mine(tokens).reshape(ROWS, WIDTH)
    my_cotangent = mine(cotangent).transpose(1, 0, 2).reshape(BLK, 2 * WIDTH)

    row_f32, row_bf16 = sds((ROWS, WIDTH), F32), sds((ROWS, WIDTH), BF16)
    packed = sds((BLK, 2 * WIDTH), BF16)
    heads_shape = sds((CTX, ROWS + BLK, 2 * HEAD), BF16)
    att_shape = sds((CTX, BLK, 2 * HEAD), BF16)
    blocks_shape = sds((FSDP, ROWS, SHARD), BF16)
    seq = lambda dtype: pltpu.VMEM((LENGTH, HEAD), dtype)
    partials = [row_f32] + [packed] * 3
    ff_f32, ff_bf16 = sds((FSDP * ROWS, FF_SHARD), F32), sds((FSDP * ROWS, FF_SHARD), BF16)
    qkv_scratch, out_scratch = row_scratch(QKV_LANES), row_scratch(OUT_LANES)
    ffn_scratch = row_scratch(2 * FF_SHARD) + [
        pltpu.VMEM((SLICES, DOWN_SLICE, FF_SHARD), BF16), pltpu.SemaphoreType.DMA,
    ]
    bind = functools.partial

    kept = []
    parts = [my_rows]
    for layer in range(2):
        gain_attn, gain_ffn = gains_of(layer)
        x, a_blocks, send = call(
            bind(qkv_body, len(parts)), [row_bf16, blocks_shape, heads_shape],
            *parts, gain_attn, cos_own, sin_own, far=[qkv_weights[layer]],
            scratch=qkv_scratch, flops=2 * ROWS * WIDTH * QKV_COLS,
        )
        if layer == 0:
            rest_weights.append(lax.all_gather(rest[0], "ctx"))
            qkv_weights.append(lax.all_gather(after(qkv[1], send), "ctx"))
        heads = all_to_all(send, "ctx")
        send = call(
            attend_body, [att_shape], heads,
            scratch=[seq(BF16), seq(BF16), seq(BF16), seq(F32)], flops=2 * LENGTH * LENGTH * HEAD,
        )[0]
        arrived = all_to_all(send, "ctx")
        if layer == 0:
            rest_weights.append(lax.all_gather(after(rest[1], arrived), "ctx"))
        else:
            first_blocks = exchange_blocks(after(kept[0][1], send), fsdp)
            arrived = after(arrived, *first_blocks)
        mixed, b, att_blocks = call(
            mix_body, [row_f32, packed, blocks_shape],
            x, arrived, gain_ffn, far=[rest_weights[layer]],
            scratch=[pltpu.VMEM((ROWS, WIDTH), BF16)] + out_scratch, flops=2 * ROWS * WIDTH * WIDTH,
        )
        b_all = around(b)
        gate, up, *outs = call(
            ffn_body, [ff_f32, ff_f32] + partials, *b_all, far=[rest_weights[layer]],
            scratch=ffn_scratch, flops=2 * FSDP * ROWS * WIDTH * FF_SHARD * 3,
        )
        if layer == 0:
            parts = [mixed] + back_around(outs)
        blocks = jnp.concatenate([a_blocks, att_blocks], axis=2)
        kept.append((x, blocks, heads, mixed, b_all, gate, up, gain_attn, gain_ffn))
    first_acts, last_outs = kept[1][0], outs

    g = my_cotangent
    ffn_grads, out_grads, d_inputs = [None, None], [None, None], [None, None]
    fsdp_index = fsdp.astype(jnp.int32).reshape(1)

    def ffn_gradient(b_all, g_all, d_gu, hidden):
        slices = call(
            ffn_grad_body, [sds((CTX, FSDP * SLICE, FFN_COLS), BF16)], *b_all, *g_all, d_gu, hidden,
            flops=2 * FSDP * ROWS * WIDTH * FFN_COLS,
        )[0]
        return lax.psum_scatter(
            slices.reshape(CTX * FSDP * SLICE, FFN_COLS), "ctx", scatter_dimension=0, tiled=True
        )

    def qkv_gradient(blocks, d_rows):
        return call(
            qkv_grad_body, [sds((CTX, SLICE, QKV_LANES), BF16)], fsdp_index, *blocks, *d_rows,
            scalars=1, flops=2 * FSDP * ROWS * SHARD * QKV_COLS,
        )[0]

    def out_gradient(blocks, ga):
        return call(
            out_grad_body, [sds((CTX, SLICE, OUT_LANES), BF16)], *blocks, *ga,
            flops=2 * FSDP * ROWS * SHARD * WIDTH,
        )[0]

    def reduced(slices):
        return all_to_all(slices, "ctx").astype(F32).sum(axis=0).astype(BF16)

    for layer in (1, 0):
        x, blocks, heads, mixed, b_all, gate, up, gain_attn, gain_ffn = kept[layer]
        g_all = around(g)
        hidden, d_gu, *outs = call(
            ffn_back_body,
            [ff_bf16, sds((FSDP * ROWS, 2 * FF_SHARD), BF16)] + partials,
            *g_all, gate, up, far=[rest_weights[layer]],
            scratch=ffn_scratch, flops=2 * FSDP * ROWS * WIDTH * FF_SHARD * 3,
        )
        if layer == 0:
            ffn_grads[0] = ffn_gradient(b_all, g_all, d_gu, hidden)
        d_mixed, ga, d_gain_ffn, send = call(
            mix_back_body, [row_f32, packed, sds((1, WIDTH), F32), att_shape],
            g, *back_around(outs), mixed, gain_ffn, far=[rest_weights[layer]],
            scratch=out_scratch, flops=2 * ROWS * WIDTH * WIDTH,
        )
        if layer == 1:
            ffn_grads[1] = ffn_gradient(b_all, g_all, after(d_gu, send), hidden)
        if layer == 1:
            blocks = exchange_blocks(after(blocks, send), fsdp)
            late_blocks = blocks
            last_parts = back_around([after(part, send) for part in last_outs])
            beside = [*blocks, *last_parts]
        else:
            blocks = first_blocks
            late_rows = around(after(d_rows, send))
            last_acts = kept[1][3] + last_parts[0]
            for part in last_parts[1:]:
                part = part.reshape(BLK, 2, WIDTH).transpose(1, 0, 2).reshape(ROWS, WIDTH)
                last_acts = last_acts + part.astype(F32)
            last_acts = last_acts.astype(BF16)
            other_acts = swap_sections(after(jnp.where(first, last_acts, first_acts), send))
            beside = [*late_rows, other_acts]
        send = call(
            attend_back_body, [heads_shape],
            heads, all_to_all(send, "ctx"), cos_all, sin_all,
            scratch=[seq(BF16)] * 4 + [seq(F32)] + [pltpu.VMEM((HEAD, LENGTH), F32)] * 2,
            flops=5 * LENGTH * LENGTH * HEAD,
        )[0]
        send = after(send, *beside)
        ga = around(after(ga, send))
        out_grads[layer] = out_gradient(blocks, ga)
        beside = [out_grads[layer]]
        if layer == 0:
            late_slices = qkv_gradient(late_blocks, late_rows)
            beside.append(late_slices)
        d_x, d_low, d_rows = call(
            qkv_back_body,
            [row_f32, packed, sds((ROWS + SLICE, QKV_LANES), BF16)],
            after(all_to_all(send, "ctx"), *beside), d_mixed, x, gain_attn, d_gain_ffn, far=[qkv_weights[layer]],
            scratch=[pltpu.VMEM((ROWS, QKV_LANES), BF16)] + qkv_scratch,
            flops=2 * ROWS * WIDTH * QKV_COLS,
        )
        d_inputs[layer] = (d_x, d_low)
        g = d_low

    def across(zero, one):
        keep, give = jnp.where(first, zero, one), jnp.where(first, one, zero)
        return (keep.astype(F32) + swap_sections(give).astype(F32)).astype(BF16)

    late_slices = reduced(jnp.concatenate([late_slices, *out_grads], axis=2))
    other_grads = swap_sections(jnp.where(first, d_inputs[1][1], d_inputs[0][1]))
    ffn_slices = across(*[after(grad, send) for grad in ffn_grads])
    gate_up = ffn_slices[:, : 2 * FF_SHARD].reshape(FSDP, SLICE, 2 * FF_SHARD)
    gate_up = jnp.concatenate(exchange_blocks(gate_up, fsdp))
    ffn_slices = jnp.concatenate([gate_up, ffn_slices[:, 2 * FF_SHARD :]], axis=1)
    out_grads = [late_slices[:, start : start + OUT_LANES] for start in (QKV_LANES, QKV_LANES + OUT_LANES)]
    d_rows = around(d_rows)
    d_rows[0] = after(d_rows[0], late_slices, other_grads, ffn_slices)
    slices = qkv_gradient(blocks, d_rows)
    out_slices = across(*[after(grad, slices) for grad in out_grads])
    qkv_slices = across(reduced(slices), late_slices[:, :QKV_LANES])
    out_slices = jnp.pad(out_slices, ((0, 0), (0, FFN_COLS - OUT_LANES)))
    gate, up, down, out = call(
        rest_result_body,
        [sds((SHARD, FF), F32), sds((SHARD, FF), F32), sds((WIDTH, FF_SHARD), F32), sds((SHARD, WIDTH), F32)],
        fsdp_index, lax.all_gather(jnp.concatenate([ffn_slices, out_slices]), "ctx"), scalars=1,
    )
    kv = KV_HEADS * HEAD
    query, key, value, gains = call(
        qkv_result_body,
        [sds((SHARD, WIDTH), F32), sds((kv, SHARD), F32), sds((kv, SHARD), F32), sds((8, SHARD), F32)],
        after(to_all(qkv_slices, "ctx", CTX), gate), scratch=[pltpu.VMEM((SHARD, 2 * kv), F32)],
    )
    other_grads = other_grads.reshape(BLK, 2, WIDTH).transpose(1, 0, 2).reshape(ROWS, WIDTH).astype(F32)
    d_one = d_inputs[1][1].reshape(BLK, 2, WIDTH).transpose(1, 0, 2).reshape(ROWS, WIDTH).astype(F32)
    mine_grads = jnp.where(first, d_inputs[0][0], d_one)
    mine_acts = jnp.where(first, first_acts, last_acts)

    def by_micro(own, other):
        pair = jnp.stack([jnp.where(first, own, other), jnp.where(first, other, own)])
        return pair.reshape(1, 2, 1, 2, BLK, WIDTH)

    return (
        by_micro(mine_acts, other_acts),
        by_micro(mine_grads, other_grads),
        gains[0:1],
        query[None],
        key.T[None],
        value.T[None],
        out[None],
        gains[1:2],
        gate[None],
        up[None],
        down.T[None],
    )


def solution(mesh):
    rows = P(None, "fsdp", None, "ctx", None)
    gain, matrix = P("section", "fsdp"), P("section", "fsdp", None)
    layer_rows = P("section", None, "fsdp", None, "ctx", None)
    weights = (gain, matrix, matrix, matrix, matrix, gain, matrix, matrix, matrix)
    return jax.shard_map(
        on_device,
        mesh=mesh,
        in_specs=(rows, rows) + weights,
        out_specs=(layer_rows, layer_rows) + weights,
        check_vma=False,
    )
```

```python
import functools

import jax
import jax.numpy as jnp
import numpy as np
from jax import lax
from jax.experimental import pallas as pl
from jax.experimental.pallas import tpu as pltpu
from jax.sharding import PartitionSpec as P

WIDTH = 960
HEADS = 15
KV_HEADS = 5
GROUP = HEADS // KV_HEADS
HEAD = 64
FF = 2560
BLK = 48
ROWS = 2 * BLK
CTX = 16
FSDP = 4
LENGTH = ROWS * CTX
SHARD = WIDTH // FSDP
FF_SHARD = FF // FSDP
QK_COLS = (HEADS + KV_HEADS) * HEAD
QKV_COLS = QK_COLS + KV_HEADS * HEAD
SLICE = 16
SLICES = SHARD // SLICE
DOWN_SLICE = WIDTH // SLICES
OUT_COLS = QKV_COLS + WIDTH
FFN_COLS = 3 * FF_SHARD
QKV_LANES = 1664
OUT_LANES = 1024
TILE = 256

EPSILON = 1e-05
THETA = 10000.0
MASKED = -1e30

F32 = jnp.float32
BF16 = jnp.bfloat16


def sds(shape, dtype):
    return jax.ShapeDtypeStruct(shape, dtype)


def call(body, outs, *args, far=(), far_out=False, wait_for=(), scalars=0, scratch=(), flops=0):
    given = len(args) + len(far)

    def kernel(*refs):
        body(*refs[:given], *refs[given + len(wait_for) :])

    size = sum(a.size * a.dtype.itemsize for a in (*args, *outs))
    specs = [pl.BlockSpec(memory_space=pltpu.SMEM if i < scalars else pltpu.VMEM) for i in range(len(args))]
    return pl.pallas_call(
        kernel,
        out_shape=outs,
        out_specs=[pl.BlockSpec(memory_space=pl.ANY if far_out else pltpu.VMEM)] * len(outs),
        in_specs=specs + [pl.BlockSpec(memory_space=pl.ANY)] * (len(far) + len(wait_for)),
        scratch_shapes=list(scratch),
        compiler_params=pltpu.CompilerParams(vmem_limit_bytes=56 * 1024 * 1024),
        cost_estimate=pl.CostEstimate(flops=flops, bytes_accessed=size, transcendentals=0),
    )(*args, *far, *wait_for)


def dot(a, b):
    return jnp.dot(a, b, preferred_element_type=F32)


def dot_t(a, b):
    return lax.dot_general(a, b, (((1,), (1,)), ((), ())), preferred_element_type=F32)


def t_dot(a, b):
    return lax.dot_general(a, b, (((0,), (0,)), ((), ())), preferred_element_type=F32)


def inverse_rms(x):
    return lax.rsqrt(jnp.mean(x * x, axis=-1, keepdims=True) + EPSILON)


def norm_backward(d, x, gain):
    r = inverse_rms(x)
    n = x * r
    t = d * gain
    return (t - n * jnp.mean(t * n, axis=-1, keepdims=True)) * r, jnp.sum(d * n, axis=0, keepdims=True)


def swap_halves(x):
    cols = x.shape[1]
    lane = lax.broadcasted_iota(jnp.int32, x.shape, 1)
    ahead = pltpu.roll(x, cols - HEAD // 2, 1)
    behind = pltpu.roll(x, HEAD // 2, 1)
    return jnp.where(lane % HEAD < HEAD // 2, ahead, behind)


def by_core(c):
    return c % 2 * (CTX // 2) + c // 2


def source_block(b):
    return (b, 0) if b < CTX else (2 * CTX - 1 - b, 1)


def rotary_constants():
    inverse = (THETA ** (-(np.arange(HEAD // 2, dtype=np.float32) * 2.0) / HEAD)).astype(np.float32)
    angles = np.arange(LENGTH, dtype=np.float32)[:, None] * inverse[None, :]
    cos, sin = np.cos(angles.astype(np.float64)), np.sin(angles.astype(np.float64))
    return (
        np.concatenate([cos] * 4, axis=1).astype(np.float32),
        np.concatenate([-sin, sin] * 2, axis=1).astype(np.float32),
    )


def pack(x):
    return jnp.concatenate([x[:BLK], x[BLK:]], axis=1)


def unpack(x):
    cols = x.shape[1] // 2
    return jnp.concatenate([x[:, :cols], x[:, cols:]], axis=0)


def load_rows(src, lanes, dst, sems):
    copies = [
        pltpu.make_async_copy(src.at[0:SLICES, f * SLICE : (f + 1) * SLICE, lanes], dst.at[f], sems.at[f])
        for f in range(FSDP)
    ]
    for copy in copies:
        copy.start()
    return copies


def load_down(src, lanes, dst, sem):
    copy = pltpu.make_async_copy(src.at[0:SLICES, :, lanes], dst, sem)
    copy.start()
    return [copy]


def wait_all(copies):
    for copy in copies:
        copy.wait()


def rows_of(scratch):
    return scratch[...].reshape(WIDTH, scratch.shape[-1])


def row_scratch(lanes):
    return [pltpu.VMEM((FSDP, SLICES, SLICE, lanes), BF16), pltpu.SemaphoreType.DMA((FSDP,))]


def qkv_body(count, start, *refs):
    parts, (gain, cos, sin, w_far) = refs[:count], refs[count : count + 4]
    x_out, a_out, send, w_s, sems = refs[count + 4 :]
    copies = load_rows(w_far, slice(start, start + QKV_LANES), w_s, sems)
    x = parts[0][...].astype(F32)
    if count > 1:
        x = x + parts[1][...]
        for part in parts[2:]:
            x = x + unpack(part[...].astype(F32))
    low = x.astype(BF16)
    x_out[...] = low
    x = low.astype(F32)
    a = x * inverse_rms(x) * gain[...]
    for k in range(FSDP):
        a_out[k] = a[:, k * SHARD : (k + 1) * SHARD].astype(BF16)
    wait_all(copies)
    out = dot(a.astype(BF16), rows_of(w_s))
    qk = out[:, :QK_COLS]
    pairs = (HEADS + KV_HEADS) // 2
    lane = lax.broadcasted_iota(jnp.int32, qk.shape, 1)
    scale = jnp.where(lane < HEADS * HEAD, HEAD**-0.5, 1.0)
    cos_all = jnp.concatenate([cos[...]] * pairs, axis=1) * scale
    sin_all = jnp.concatenate([sin[...]] * pairs, axis=1) * scale
    qk = qk * cos_all + swap_halves(qk) * sin_all
    v = out[:, QK_COLS:QKV_COLS]
    for h in range(HEADS):
        g = h // GROUP
        q_h = qk[:, h * HEAD : (h + 1) * HEAD]
        k_g = qk[:, (HEADS + g) * HEAD : (HEADS + g + 1) * HEAD]
        v_g = v[:, g * HEAD : (g + 1) * HEAD]
        send[h, 0:ROWS] = jnp.concatenate([q_h, k_g], axis=1).astype(BF16)
        send[h, ROWS:] = pack(v_g).astype(BF16)
    for h in range(HEADS, CTX):
        send[h] = jnp.zeros(send.shape[1:], BF16)


def unpack_heads(recv, q_s, k_s, v_s):
    for b in range(2 * CTX):
        c, half = source_block(b)
        rows = slice(b * BLK, (b + 1) * BLK)
        qk = recv[c, half * BLK : (half + 1) * BLK, :].astype(F32)
        v = recv[c, ROWS : ROWS + BLK, :].astype(F32)
        q_s[rows, :] = qk[:, :HEAD].astype(BF16)
        k_s[rows, :] = qk[:, HEAD:].astype(BF16)
        v_s[rows, :] = v[:, half * HEAD : (half + 1) * HEAD].astype(BF16)


def masked_scores(q, keys, start):
    scores = dot_t(q, keys)
    row = lax.broadcasted_iota(jnp.int32, (TILE, TILE), 0)
    col = lax.broadcasted_iota(jnp.int32, (TILE, TILE), 1)
    last = jnp.where(col <= row, scores[:, start:], MASKED)
    return last if start == 0 else jnp.concatenate([scores[:, :start], last], axis=1)


def attend_body(recv, send, log_out, q_s, k_s, v_s, out_s):
    unpack_heads(recv, q_s, k_s, v_s)
    for i in range(LENGTH // TILE):
        start, stop = i * TILE, (i + 1) * TILE
        scores = masked_scores(q_s[start:stop, :], k_s[:stop, :], start)
        top = jnp.max(scores, axis=-1, keepdims=True)
        weights = jnp.exp(scores - top)
        total = jnp.sum(weights, axis=-1, keepdims=True)
        log_out[start:stop, :] = top + jnp.log(total)
        p = weights * (1.0 / total)
        out_s[start:stop, :] = dot(p.astype(BF16), v_s[:stop, :])
    for c in range(CTX):
        last = 2 * CTX - 1 - c
        pair = [out_s[c * BLK : (c + 1) * BLK, :], out_s[last * BLK : (last + 1) * BLK, :]]
        send[c] = jnp.concatenate(pair, axis=1).astype(BF16)


def mix_body(start, x, recv, gain, w_far, mixed_out, b_out, att_out, att_s, w_s, sems):
    copies = load_rows(w_far, slice(start, start + OUT_LANES), w_s, sems)
    for h in range(HEADS):
        pair = recv[h].astype(F32)
        cols = slice(h * HEAD, (h + 1) * HEAD)
        att_s[0:BLK, cols] = pair[:, :HEAD].astype(BF16)
        att_s[BLK:, cols] = pair[:, HEAD:].astype(BF16)
    att = att_s[...]
    for k in range(FSDP):
        att_out[k] = att_s[:, k * SHARD : (k + 1) * SHARD]
    wait_all(copies)
    mixed = x[...].astype(F32) + dot(att, rows_of(w_s))[:, :WIDTH]
    mixed_out[...] = mixed
    b_out[...] = pack(mixed * inverse_rms(mixed) * gain[...]).astype(BF16)


def spread(total, outs):
    outs[0][...] = total[0:ROWS]
    for k in range(1, FSDP):
        outs[k][...] = pack(total[k * ROWS : (k + 1) * ROWS]).astype(BF16)


def all_rows(parts):
    return jnp.concatenate([unpack(p[...]) for p in parts], axis=0)


def ffn_body(start, *refs):
    parts, w_far, (gate_out, up_out), outs = refs[:4], refs[4], refs[5:7], refs[7:11]
    w_s, sems, down_s, down_sem = refs[11:]
    copies = load_rows(w_far, slice(start, start + 2 * FF_SHARD), w_s, sems)
    down = load_down(w_far, slice(start + 2 * FF_SHARD, start + FFN_COLS), down_s, down_sem)
    rows = all_rows(parts)
    wait_all(copies)
    gate_up = dot(rows, rows_of(w_s))
    gate, up = gate_up[:, :FF_SHARD], gate_up[:, FF_SHARD:]
    gate_out[...] = gate
    up_out[...] = up
    hidden = (gate * jax.nn.sigmoid(gate) * up).astype(BF16)
    wait_all(down)
    spread(dot_t(hidden, rows_of(down_s)), outs)


def ffn_back_body(start, *refs):
    parts, (gate_ref, up_ref, w_far) = refs[:4], refs[4:7]
    hidden_out, d_gu_out = refs[7:9]
    outs = refs[9:13]
    w_s, sems, down_s, down_sem = refs[13:]
    down = load_down(w_far, slice(start + 2 * FF_SHARD, start + FFN_COLS), down_s, down_sem)
    copies = load_rows(w_far, slice(start, start + 2 * FF_SHARD), w_s, sems)
    rows = all_rows(parts)
    gate, up = gate_ref[...], up_ref[...]
    sig = jax.nn.sigmoid(gate)
    act = gate * sig
    hidden_out[...] = (act * up).astype(BF16)
    wait_all(down)
    d_hidden = dot(rows, rows_of(down_s))
    d_gu_out[:, :FF_SHARD] = (d_hidden * up * (sig * (1.0 + gate * (1.0 - sig)))).astype(BF16)
    d_gu_out[:, FF_SHARD:] = (d_hidden * act).astype(BF16)
    wait_all(copies)
    spread(dot_t(d_gu_out[...], rows_of(w_s)), outs)


def ffn_grad_body(*refs):
    b_parts, g_parts, d_gu, hidden, out = refs[:4], refs[4:8], refs[8], refs[9], refs[10]
    stage, sems = refs[11:]
    for c in range(SLICES, CTX):
        stage[c] = jnp.zeros(stage.shape[1:], BF16)
    rows = all_rows(b_parts)
    copies = []
    for group in range(3):
        lanes = slice(group * FF_SHARD, (group + 1) * FF_SHARD)
        if group < 2:
            grad = t_dot(rows, d_gu[:, lanes]).astype(BF16)
            for f in range(FSDP):
                for c in range(SLICES):
                    first = f * SHARD + c * SLICE
                    stage[c, f * SLICE : (f + 1) * SLICE, lanes] = grad[first : first + SLICE]
        else:
            grad = t_dot(all_rows(g_parts), hidden[...]).astype(BF16)
            for c in range(SLICES):
                stage[c, :, lanes] = grad[c * DOWN_SLICE : (c + 1) * DOWN_SLICE]
        copies.append(pltpu.make_async_copy(stage.at[:, :, lanes], out.at[:, :, lanes], sems.at[group]))
        copies[-1].start()
    wait_all(copies)


def mix_back_body(start, g, p0, p1, p2, p3, mixed, gain, w_far, d_mixed_out, ga_out, gain_out, send, w_s, sems):
    copies = load_rows(w_far, slice(start, start + OUT_LANES), w_s, sems)
    d_b = p0[...]
    for part in (p1, p2, p3):
        d_b = d_b + unpack(part[...].astype(F32))
    d_in, d_gain = norm_backward(d_b, mixed[...], gain[...])
    d_mixed = unpack(g[...].astype(F32)) + d_in
    d_mixed_out[...] = d_mixed
    gain_out[...] = d_gain
    ga_out[...] = pack(d_mixed).astype(BF16)
    wide = jnp.concatenate([d_mixed, jnp.zeros((ROWS, OUT_LANES - WIDTH), F32)], axis=1).astype(BF16)
    wait_all(copies)
    d_att = dot_t(wide, rows_of(w_s))
    for h in range(HEADS):
        send[h] = pack(d_att[:, h * HEAD : (h + 1) * HEAD]).astype(BF16)
    for h in range(HEADS, CTX):
        send[h] = jnp.zeros(send.shape[1:], BF16)


def attend_back_body(recv, d_recv, log_total, cos, sin, send, q_s, k_s, v_s, d_s, dq_s, dk_s, dv_s):
    unpack_heads(recv, q_s, k_s, v_s)
    for b in range(2 * CTX):
        c, half = source_block(b)
        pair = d_recv[c].astype(F32)
        d_s[b * BLK : (b + 1) * BLK, :] = pair[:, half * HEAD : (half + 1) * HEAD].astype(BF16)
    dk_s[...] = jnp.zeros(dk_s.shape, F32)
    dv_s[...] = jnp.zeros(dv_s.shape, F32)
    for i in range(LENGTH // TILE):
        start, stop = i * TILE, (i + 1) * TILE
        q, d_att = q_s[start:stop, :], d_s[start:stop, :]
        p = jnp.exp(masked_scores(q, k_s[:stop, :], start) - log_total[start:stop, :])
        d_p = dot_t(d_att, v_s[:stop, :])
        inner = jnp.sum(p * d_p, axis=-1, keepdims=True)
        d_scores = (p * (d_p - inner)).astype(BF16)
        dq_s[start:stop, :] = dot(d_scores, k_s[:stop, :])
        dk_s[:, :stop] += t_dot(q, d_scores)
        dv_s[:, :stop] += t_dot(d_att, p.astype(BF16))
    dk = dk_s[...].T
    dv = dv_s[...].T
    both = jnp.concatenate([dq_s[...] * (HEAD**-0.5), dk], axis=1)
    both = both * cos[...] - swap_halves(both) * sin[...]
    for c in range(CTX):
        last = 2 * CTX - 1 - c
        send[c, 0:BLK] = both[c * BLK : (c + 1) * BLK].astype(BF16)
        send[c, BLK:ROWS] = both[last * BLK : (last + 1) * BLK].astype(BF16)
        pair = [dv[c * BLK : (c + 1) * BLK], dv[last * BLK : (last + 1) * BLK]]
        send[c, ROWS:] = jnp.concatenate(pair, axis=1).astype(BF16)


def qkv_back_body(start, recv, d_mixed, x_ref, gain, gain_ffn, w_far, d_x_out, low_out, rows_out, rows_s, w_s, sems):
    copies = load_rows(w_far, slice(start, start + QKV_LANES), w_s, sems)
    rows_s[:, QKV_COLS:] = jnp.zeros((ROWS, QKV_LANES - QKV_COLS), BF16)
    for g in range(KV_HEADS):
        d_k = jnp.zeros((ROWS, HEAD), F32)
        d_v = jnp.zeros((BLK, 2 * HEAD), F32)
        for h in range(g * GROUP, (g + 1) * GROUP):
            qk = recv[h, 0:ROWS].astype(F32)
            rows_s[:, h * HEAD : (h + 1) * HEAD] = qk[:, :HEAD].astype(BF16)
            d_k = d_k + qk[:, HEAD:]
            d_v = d_v + recv[h, ROWS:].astype(F32)
        k_cols = slice((HEADS + g) * HEAD, (HEADS + g + 1) * HEAD)
        v_cols = slice(QK_COLS + g * HEAD, QK_COLS + (g + 1) * HEAD)
        rows_s[:, k_cols] = d_k.astype(BF16)
        rows_s[:, v_cols] = unpack(d_v).astype(BF16)
    rows = rows_s[...]
    rows_out[0:ROWS] = rows
    wait_all(copies)
    d_a = dot_t(rows, rows_of(w_s))
    d_in, d_gain = norm_backward(d_a, x_ref[...].astype(F32), gain[...])
    d_x = d_mixed[...] + d_in
    d_x_out[...] = d_x
    low_out[...] = pack(d_x).astype(BF16)
    gains = jnp.concatenate([d_gain, gain_ffn[...], jnp.zeros((SLICE - 2, WIDTH), F32)], axis=0)
    gains = jnp.concatenate([gains, jnp.zeros((SLICE, QKV_LANES - WIDTH), F32)], axis=1)
    rows_out[ROWS:] = gains.astype(BF16)


def qkv_grad_body(fsdp_ref, *refs):
    blocks, parts, others, out = refs[:4], refs[4:8], refs[8:-1], refs[-1]
    start = QKV_LANES
    for other in others:
        out[:, :, start : start + other.shape[2]] = other[...]
        start += other.shape[2]
    cols = jnp.concatenate([p[:, :SHARD] for p in blocks], axis=0)
    rows = jnp.concatenate([p[0:ROWS] for p in parts], axis=0)
    grad = t_dot(cols, rows).astype(BF16)
    for c in range(SLICES):
        out[by_core(c), :, :QKV_LANES] = grad[c * SLICE : (c + 1) * SLICE]
    gains = sum(p[ROWS:].astype(F32) for p in parts)
    mine = jnp.zeros((SLICE, SHARD), F32)
    for f in range(FSDP):
        mine = jnp.where(fsdp_ref[0] == f, gains[:, f * SHARD : (f + 1) * SHARD], mine)
    mine = jnp.concatenate([mine, jnp.zeros((SLICE, QKV_LANES - SHARD), F32)], axis=1)
    out[by_core(SLICES), :, :QKV_LANES] = mine.astype(BF16)


def out_grad_body(*refs):
    blocks, ga_parts, out = refs[:4], refs[4:8], refs[8]
    cols = jnp.concatenate([p[:, SHARD:] for p in blocks], axis=0)
    grad = t_dot(cols, all_rows(ga_parts))
    grad = jnp.concatenate([grad, jnp.zeros((SHARD, OUT_LANES - WIDTH), F32)], axis=1).astype(BF16)
    for c in range(SLICES):
        out[by_core(c)] = grad[c * SLICE : (c + 1) * SLICE]
    out[by_core(SLICES)] = jnp.zeros((SLICE, OUT_LANES), BF16)


def rest_result_body(fsdp_ref, gathered, gate, up, down, out):
    for c in range(SLICES):
        rows = slice(c * SLICE, (c + 1) * SLICE)
        for k in range(FSDP):
            member = lax.rem(fsdp_ref[0] + FSDP - k, FSDP)
            cols = pl.ds(pl.multiple_of(member * FF_SHARD, 128), FF_SHARD)
            piece = gathered[c, k * SLICE : (k + 1) * SLICE, : 2 * FF_SHARD].astype(F32)
            gate[rows, cols] = piece[:, :FF_SHARD]
            up[rows, cols] = piece[:, FF_SHARD:]
        out[rows] = gathered[c, FSDP * SLICE :, :WIDTH].astype(F32)
        down[c * DOWN_SLICE : (c + 1) * DOWN_SLICE] = gathered[c, 0 : FSDP * SLICE, 2 * FF_SHARD : FFN_COLS].astype(F32)


def qkv_result_body(core_ref, same, other, query, key, value, gains, kv_s):
    kv = KV_HEADS * HEAD
    swapped = core_ref[0] == 1
    gathered = []
    for c in range(CTX):
        here, there = (same, other) if c % 2 == 0 else (other, same)
        gathered.append(jnp.where(swapped, there[c // 2], here[c // 2]))
    for c in range(SLICES):
        rows = slice(c * SLICE, (c + 1) * SLICE)
        piece = gathered[c].astype(F32)
        query[rows] = piece[:, :WIDTH]
        kv_s[rows] = piece[:, WIDTH:QKV_COLS]
    turned = kv_s[...].T
    key[...] = turned[:kv]
    value[...] = turned[kv:]
    gains[...] = gathered[SLICES][:8, :SHARD].astype(F32)


def shifted(x, axis, distance):
    n = lax.axis_size(axis)
    return lax.ppermute(x, axis, [(i, (i + distance) % n) for i in range(n)])


def around(x):
    return [x] + [shifted(x, "fsdp", k) for k in range(1, FSDP)]


def back_around(parts):
    return [parts[0]] + [shifted(parts[k], "fsdp", -k) for k in range(1, FSDP)]


def exchange_blocks(blocks, index):
    pick = lambda k: lax.dynamic_index_in_dim(blocks, (index + k) % FSDP, 0, keepdims=False)
    return [pick(0)] + [shifted(pick(k), "fsdp", k) for k in range(1, FSDP)]


def swap_sections(x):
    return lax.ppermute(x, "section", [(0, 1), (1, 0)])


def all_to_all(x, axis):
    return lax.all_to_all(x, axis, 0, 0)


def after(x, *earlier):
    return lax.optimization_barrier((x, earlier))[0]


def core_pair(x):
    return lax.ppermute(x, "ctx", [(i, i ^ 1) for i in range(CTX)])


def same_core(x):
    return lax.all_to_all(x, "ctx", 0, 0, axis_index_groups=[list(range(k, CTX, 2)) for k in range(2)])


def to_all(x, axis, count):
    return all_to_all(jnp.broadcast_to(x[None], (count,) + x.shape), axis)


def on_device(
    tokens,
    cotangent,
    norm_attn,
    w_query,
    key_projection,
    value_projection,
    w_out,
    norm_ffn,
    w_gate,
    w_up,
    w_down,
):
    section = lax.axis_index("section")
    ctx = lax.axis_index("ctx")
    fsdp = lax.axis_index("fsdp")
    first = section == 0

    place = jnp.minimum(ctx, SLICES - 1)

    def my_slice(rows, count=SLICE):
        return lax.dynamic_slice_in_dim(rows, place * count, count, 0)

    own_gains = jnp.concatenate([norm_attn, norm_ffn], axis=1)
    own_gains = jnp.pad(own_gains, ((0, SLICE - 1), (0, QKV_LANES + OUT_LANES - 2 * SHARD)))
    own = [my_slice(w[0]) for w in (w_query, key_projection, value_projection)]
    own.append(jnp.zeros((SLICE, QKV_LANES - QKV_COLS), BF16))
    own += [my_slice(w_out[0]), jnp.zeros((SLICE, OUT_LANES - WIDTH), BF16)]
    own = jnp.where(ctx < SLICES, jnp.concatenate(own, axis=1), own_gains)
    attention = to_all(own, ("section", "fsdp"), 2 * FSDP).reshape(2, FSDP * SLICE, QKV_LANES + OUT_LANES)

    ffn = [my_slice(w[0]).reshape(SLICE, FSDP, FF_SHARD) for w in (w_gate, w_up)]
    ffn = jnp.concatenate(ffn, axis=2).transpose(1, 0, 2)
    ffn = all_to_all(after(jnp.concatenate([ffn, ffn]), attention), ("section", "fsdp"))
    ffn = ffn.reshape(2, FSDP * SLICE, 2 * FF_SHARD)
    down = my_slice(w_down[0].T, DOWN_SLICE)
    down_other = swap_sections(after(down, attention))
    downs = (jnp.where(first, down, down_other), jnp.where(first, down_other, down))
    ffn = [jnp.concatenate(pair, axis=1) for pair in zip(ffn, downs)]

    gathered = lax.all_gather(attention[0], "ctx")
    qkv_weights, out_weights = [(gathered, 0)], [(gathered, QKV_LANES)]
    ffn_weights = []

    def gains_of(layer):
        source, start = qkv_weights[layer]
        rows = source[SLICES, ::SLICE, start : start + 2 * SHARD].astype(F32)
        return rows[:, :SHARD].reshape(1, WIDTH), rows[:, SHARD:].reshape(1, WIDTH)

    cos_all, sin_all = rotary_constants()
    cos_all, sin_all = jnp.asarray(cos_all), jnp.asarray(sin_all)

    def own_positions(table):
        pieces = [
            lax.dynamic_slice_in_dim(table, start * BLK, BLK, 0) for start in (ctx, 2 * CTX - 1 - ctx)
        ]
        return jnp.concatenate(pieces)

    cos_own, sin_own = own_positions(cos_all), own_positions(sin_all)

    def mine(x):
        return lax.dynamic_index_in_dim(x, section, 0, keepdims=False).reshape(2, BLK, WIDTH)

    my_rows = mine(tokens).reshape(ROWS, WIDTH)
    my_cotangent = mine(cotangent).transpose(1, 0, 2).reshape(BLK, 2 * WIDTH)

    row_f32, row_bf16 = sds((ROWS, WIDTH), F32), sds((ROWS, WIDTH), BF16)
    packed = sds((BLK, 2 * WIDTH), BF16)
    heads_shape = sds((CTX, ROWS + BLK, 2 * HEAD), BF16)
    att_shape = sds((CTX, BLK, 2 * HEAD), BF16)
    blocks_shape = sds((FSDP, ROWS, SHARD), BF16)
    seq = lambda dtype: pltpu.VMEM((LENGTH, HEAD), dtype)
    partials = [row_f32] + [packed] * 3
    ff_f32, ff_bf16 = sds((FSDP * ROWS, FF_SHARD), F32), sds((FSDP * ROWS, FF_SHARD), BF16)
    qkv_scratch, out_scratch = row_scratch(QKV_LANES), row_scratch(OUT_LANES)
    ffn_scratch = row_scratch(2 * FF_SHARD) + [
        pltpu.VMEM((SLICES, DOWN_SLICE, FF_SHARD), BF16), pltpu.SemaphoreType.DMA,
    ]
    bind = functools.partial

    kept = []
    parts = [my_rows]
    for layer in range(2):
        qkv_w, qkv_at = qkv_weights[layer]
        gain_attn, gain_ffn = gains_of(layer)
        x, a_blocks, send = call(
            bind(qkv_body, len(parts), qkv_at), [row_bf16, blocks_shape, heads_shape],
            *parts, gain_attn, cos_own, sin_own, far=[qkv_w],
            scratch=qkv_scratch, flops=2 * ROWS * WIDTH * QKV_COLS,
        )
        if layer == 0:
            gathered = jnp.concatenate([ffn[0], attention[1][:, :QKV_LANES]], axis=1)
            gathered = lax.all_gather(gathered, "ctx")
            ffn_weights.append((gathered, 0))
            qkv_weights.append((gathered, FFN_COLS))
        heads = all_to_all(send, "ctx")
        beside = []
        if layer == 1:
            first_blocks = exchange_blocks(after(kept[0][1], send), fsdp)
            beside = first_blocks
        send, log_total = call(
            attend_body, [att_shape, sds((LENGTH, 1), F32)], heads,
            wait_for=beside, scratch=[seq(BF16), seq(BF16), seq(BF16), seq(F32)], flops=2 * LENGTH * LENGTH * HEAD,
        )
        arrived = all_to_all(send, "ctx")
        if layer == 0:
            gathered = jnp.concatenate([ffn[1], attention[1][:, QKV_LANES:]], axis=1)
            gathered = lax.all_gather(after(gathered, arrived), "ctx")
            ffn_weights.append((gathered, 0))
            out_weights.append((gathered, FFN_COLS))
        (out_w, out_at), (ffn_w, ffn_at) = out_weights[layer], ffn_weights[layer]
        mixed, b, att_blocks = call(
            bind(mix_body, out_at), [row_f32, packed, blocks_shape],
            x, arrived, gain_ffn, far=[out_w],
            scratch=[pltpu.VMEM((ROWS, WIDTH), BF16)] + out_scratch, flops=2 * ROWS * WIDTH * WIDTH,
        )
        b_all = around(b)
        gate, up, *outs = call(
            bind(ffn_body, ffn_at), [ff_f32, ff_f32] + partials, *b_all, far=[ffn_w],
            scratch=ffn_scratch, flops=2 * FSDP * ROWS * WIDTH * FF_SHARD * 3,
        )
        if layer == 0:
            parts = [mixed] + back_around(outs)
        blocks = jnp.concatenate([a_blocks, att_blocks], axis=2)
        kept.append((x, blocks, heads, log_total, mixed, b_all, gate, up, gain_attn, gain_ffn))
    first_acts, last_outs = kept[1][0], outs

    g = my_cotangent
    ffn_grads, out_grads, d_inputs = [None, None], [None, None], [None, None]
    fsdp_index = fsdp.astype(jnp.int32).reshape(1)

    def ffn_gradient(b_all, g_all, d_gu, hidden):
        slices = call(
            ffn_grad_body, [sds((CTX, FSDP * SLICE, FFN_COLS), BF16)], *b_all, *g_all, d_gu, hidden, far_out=True,
            scratch=[pltpu.VMEM((CTX, FSDP * SLICE, FFN_COLS), BF16), pltpu.SemaphoreType.DMA((3,))],
            flops=2 * FSDP * ROWS * WIDTH * FFN_COLS,
        )[0]
        return slices.reshape(CTX * FSDP * SLICE, FFN_COLS)

    def qkv_gradient(blocks, d_rows, *others, wait_for=()):
        lanes = QKV_LANES + sum(other.shape[2] for other in others)
        return call(
            qkv_grad_body, [sds((CTX, SLICE, lanes), BF16)], fsdp_index, *blocks, *d_rows, *others,
            wait_for=wait_for, scalars=1, flops=2 * FSDP * ROWS * SHARD * QKV_COLS,
        )[0]

    def out_gradient(blocks, ga):
        return call(
            out_grad_body, [sds((CTX, SLICE, OUT_LANES), BF16)], *blocks, *ga,
            flops=2 * FSDP * ROWS * SHARD * WIDTH,
        )[0]

    def reduced(slices):
        halves = slices.reshape(2, CTX // 2, *slices.shape[1:])
        keep, give = [lax.dynamic_index_in_dim(halves, k, 0, keepdims=False) for k in (ctx % 2, 1 - ctx % 2)]
        half = (keep.astype(F32) + core_pair(give).astype(F32)).astype(BF16)
        return same_core(half).astype(F32).sum(axis=0).astype(BF16)

    for layer in (1, 0):
        x, blocks, heads, log_total, mixed, b_all, gate, up, gain_attn, gain_ffn = kept[layer]
        (qkv_w, qkv_at), (out_w, out_at), (ffn_w, ffn_at) = qkv_weights[layer], out_weights[layer], ffn_weights[layer]
        g_all = around(g)
        hidden, d_gu, *outs = call(
            bind(ffn_back_body, ffn_at),
            [ff_bf16, sds((FSDP * ROWS, 2 * FF_SHARD), BF16)] + partials,
            *g_all, gate, up, far=[ffn_w],
            scratch=ffn_scratch, flops=2 * FSDP * ROWS * WIDTH * FF_SHARD * 3,
        )
        arrived = back_around(outs)
        slices = ffn_gradient(b_all, g_all, d_gu, hidden)
        ffn_grads[layer] = lax.psum_scatter(slices, "ctx", scatter_dimension=0, tiled=True)
        d_mixed, ga, d_gain_ffn, send = call(
            bind(mix_back_body, out_at), [row_f32, packed, sds((1, WIDTH), F32), att_shape],
            g, *arrived, mixed, gain_ffn, far=[out_w], wait_for=[slices],
            scratch=out_scratch, flops=2 * ROWS * WIDTH * WIDTH,
        )
        if layer == 1:
            ga = around(after(ga, send))
            beside = ga
        else:
            late_rows = around(after(d_rows, send))
            last_acts = kept[1][4] + last_parts[0]
            for part in last_parts[1:]:
                part = part.reshape(BLK, 2, WIDTH).transpose(1, 0, 2).reshape(ROWS, WIDTH)
                last_acts = last_acts + part.astype(F32)
            last_acts = last_acts.astype(BF16)
            other_acts = swap_sections(after(jnp.where(first, last_acts, first_acts), send))
            beside = [*late_rows, other_acts]
        send = call(
            attend_back_body, [heads_shape],
            heads, all_to_all(send, "ctx"), log_total, cos_all, sin_all,
            scratch=[seq(BF16)] * 4 + [seq(F32)] + [pltpu.VMEM((HEAD, LENGTH), F32)] * 2,
            flops=5 * LENGTH * LENGTH * HEAD,
        )[0]
        send = after(send, *beside)
        if layer == 1:
            blocks = exchange_blocks(after(blocks, send), fsdp)
            last_parts = back_around([after(part, send) for part in last_outs])
            out_grads[1] = out_gradient(blocks, ga)
            beside, late_blocks = [*last_parts, out_grads[1]], blocks
        else:
            blocks = first_blocks
            ga = around(after(ga, send))
            late_slices = qkv_gradient(late_blocks, late_rows)
            out_grads[0] = out_gradient(blocks, ga)
            beside = [late_slices, out_grads[0]]
        d_x, d_low, d_rows = call(
            bind(qkv_back_body, qkv_at),
            [row_f32, packed, sds((ROWS + SLICE, QKV_LANES), BF16)],
            all_to_all(send, "ctx"), d_mixed, x, gain_attn, d_gain_ffn, far=[qkv_w], wait_for=beside,
            scratch=[pltpu.VMEM((ROWS, QKV_LANES), BF16)] + qkv_scratch,
            flops=2 * ROWS * WIDTH * QKV_COLS,
        )
        d_inputs[layer] = (d_x, d_low)
        g = d_low

    def across(zero, one):
        keep, give = jnp.where(first, zero, one), jnp.where(first, one, zero)
        return (keep.astype(F32) + swap_sections(give).astype(F32)).astype(BF16)

    late_slices = reduced(after(jnp.concatenate([late_slices, *out_grads], axis=2), d_rows))
    d_rows = around(d_rows)
    ffn_slices = across(*[after(grad, d_rows[0]) for grad in ffn_grads])
    gate_up = ffn_slices[:, : 2 * FF_SHARD].reshape(FSDP, SLICE, 2 * FF_SHARD)
    gate_up = jnp.concatenate(exchange_blocks(gate_up, fsdp))
    ffn_slices = jnp.concatenate([gate_up, ffn_slices[:, 2 * FF_SHARD :]], axis=1)
    slices = qkv_gradient(blocks, d_rows, wait_for=[late_slices, ffn_slices])
    out_grads = [late_slices[:, start : start + OUT_LANES] for start in (QKV_LANES, QKV_LANES + OUT_LANES)]
    out_slices = jnp.pad(across(*[after(grad, slices) for grad in out_grads]), ((0, 0), (0, FFN_COLS - OUT_LANES)))
    rest_slices = jnp.concatenate([ffn_slices, out_slices])
    other_grads = swap_sections(after(jnp.where(first, d_inputs[1][1], d_inputs[0][1]), slices))
    qkv_slices = across(reduced(slices), late_slices[:, :QKV_LANES])
    gate, up, down, out = call(
        rest_result_body,
        [sds((SHARD, FF), F32), sds((SHARD, FF), F32), sds((WIDTH, FF_SHARD), F32), sds((SHARD, WIDTH), F32)],
        fsdp_index, lax.all_gather(rest_slices, "ctx"), scalars=1,
    )
    kv = KV_HEADS * HEAD
    qkv_same = same_core(jnp.broadcast_to(qkv_slices[None], (CTX // 2,) + qkv_slices.shape))
    query, key, value, gains = call(
        qkv_result_body,
        [sds((SHARD, WIDTH), F32), sds((kv, SHARD), F32), sds((kv, SHARD), F32), sds((8, SHARD), F32)],
        (ctx % 2).astype(jnp.int32).reshape(1), qkv_same, core_pair(qkv_same),
        scratch=[pltpu.VMEM((SHARD, 2 * kv), F32)], scalars=1, wait_for=[gate, other_grads],
    )
    other_grads = other_grads.reshape(BLK, 2, WIDTH).transpose(1, 0, 2).reshape(ROWS, WIDTH).astype(F32)
    d_one = d_inputs[1][1].reshape(BLK, 2, WIDTH).transpose(1, 0, 2).reshape(ROWS, WIDTH).astype(F32)
    mine_grads = jnp.where(first, d_inputs[0][0], d_one)
    mine_acts = jnp.where(first, first_acts, last_acts)

    def by_micro(own, other):
        pair = jnp.stack([jnp.where(first, own, other), jnp.where(first, other, own)])
        return pair.reshape(1, 2, 1, 2, BLK, WIDTH)

    return (
        by_micro(mine_acts, other_acts),
        by_micro(mine_grads, other_grads),
        gains[0:1],
        query[None],
        key.T[None],
        value.T[None],
        out[None],
        gains[1:2],
        gate[None],
        up[None],
        down.T[None],
    )


def solution(mesh):
    rows = P(None, "fsdp", None, "ctx", None)
    gain, matrix = P("section", "fsdp"), P("section", "fsdp", None)
    layer_rows = P("section", None, "fsdp", None, "ctx", None)
    weights = (gain, matrix, matrix, matrix, matrix, gain, matrix, matrix, matrix)
    return jax.shard_map(
        on_device,
        mesh=mesh,
        in_specs=(rows, rows) + weights,
        out_specs=(layer_rows, layer_rows) + weights,
        check_vma=False,
    )
```

```python
import functools

import jax
import jax.numpy as jnp
import numpy as np
from jax import lax
from jax.experimental import pallas as pl
from jax.experimental.pallas import tpu as pltpu
from jax.sharding import PartitionSpec as P

WIDTH = 960
HEADS = 15
KV_HEADS = 5
GROUP = HEADS // KV_HEADS
HEAD = 64
FF = 2560
BLK = 48
ROWS = 2 * BLK
CTX = 16
FSDP = 4
LENGTH = ROWS * CTX
SHARD = WIDTH // FSDP
FF_SHARD = FF // FSDP
QK_COLS = (HEADS + KV_HEADS) * HEAD
QKV_COLS = QK_COLS + KV_HEADS * HEAD
SLICE = 16
SLICES = SHARD // SLICE
DOWN_SLICE = WIDTH // SLICES
OUT_COLS = QKV_COLS + WIDTH
FFN_COLS = 3 * FF_SHARD
QKV_LANES = 1664
OUT_LANES = 1024
TILE = 256

EPSILON = 1e-05
THETA = 10000.0
MASKED = -1e30

F32 = jnp.float32
BF16 = jnp.bfloat16


def sds(shape, dtype):
    return jax.ShapeDtypeStruct(shape, dtype)


def call(body, outs, *args, far=(), far_out=False, wait_for=(), scalars=0, scratch=(), flops=0):
    given = len(args) + len(far)

    def kernel(*refs):
        body(*refs[:given], *refs[given + len(wait_for) :])

    size = sum(a.size * a.dtype.itemsize for a in (*args, *outs))
    specs = [pl.BlockSpec(memory_space=pltpu.SMEM if i < scalars else pltpu.VMEM) for i in range(len(args))]
    return pl.pallas_call(
        kernel,
        out_shape=outs,
        out_specs=[pl.BlockSpec(memory_space=pl.ANY if far_out else pltpu.VMEM)] * len(outs),
        in_specs=specs + [pl.BlockSpec(memory_space=pl.ANY)] * (len(far) + len(wait_for)),
        scratch_shapes=list(scratch),
        compiler_params=pltpu.CompilerParams(vmem_limit_bytes=56 * 1024 * 1024),
        cost_estimate=pl.CostEstimate(flops=flops, bytes_accessed=size, transcendentals=0),
    )(*args, *far, *wait_for)


def dot(a, b):
    return jnp.dot(a, b, preferred_element_type=F32)


def dot_t(a, b):
    return lax.dot_general(a, b, (((1,), (1,)), ((), ())), preferred_element_type=F32)


def t_dot(a, b):
    return lax.dot_general(a, b, (((0,), (0,)), ((), ())), preferred_element_type=F32)


def inverse_rms(x):
    return lax.rsqrt(jnp.mean(x * x, axis=-1, keepdims=True) + EPSILON)


def norm_backward(d, x, gain):
    r = inverse_rms(x)
    n = x * r
    t = d * gain
    return (t - n * jnp.mean(t * n, axis=-1, keepdims=True)) * r, jnp.sum(d * n, axis=0, keepdims=True)


def swap_halves(x):
    cols = x.shape[1]
    lane = lax.broadcasted_iota(jnp.int32, x.shape, 1)
    ahead = pltpu.roll(x, cols - HEAD // 2, 1)
    behind = pltpu.roll(x, HEAD // 2, 1)
    return jnp.where(lane % HEAD < HEAD // 2, ahead, behind)


def by_core(c):
    return c % 2 * (CTX // 2) + c // 2


def source_block(b):
    return (b, 0) if b < CTX else (2 * CTX - 1 - b, 1)


def rotary_constants():
    inverse = (THETA ** (-(np.arange(HEAD // 2, dtype=np.float32) * 2.0) / HEAD)).astype(np.float32)
    angles = np.arange(LENGTH, dtype=np.float32)[:, None] * inverse[None, :]
    cos, sin = np.cos(angles.astype(np.float64)), np.sin(angles.astype(np.float64))
    return (
        np.concatenate([cos] * 4, axis=1).astype(np.float32),
        np.concatenate([-sin, sin] * 2, axis=1).astype(np.float32),
    )


def pack(x):
    return jnp.concatenate([x[:BLK], x[BLK:]], axis=1)


def unpack(x):
    cols = x.shape[1] // 2
    return jnp.concatenate([x[:, :cols], x[:, cols:]], axis=0)


def load_rows(src, lanes, dst, sems):
    copies = [
        pltpu.make_async_copy(src.at[0:SLICES, f * SLICE : (f + 1) * SLICE, lanes], dst.at[f], sems.at[f])
        for f in range(FSDP)
    ]
    for copy in copies:
        copy.start()
    return copies


def load_down(src, lanes, dst, sem):
    copy = pltpu.make_async_copy(src.at[0:SLICES, :, lanes], dst, sem)
    copy.start()
    return [copy]


def wait_all(copies):
    for copy in copies:
        copy.wait()


def rows_of(scratch):
    return scratch[...].reshape(WIDTH, scratch.shape[-1])


def row_scratch(lanes):
    return [pltpu.VMEM((FSDP, SLICES, SLICE, lanes), BF16), pltpu.SemaphoreType.DMA((FSDP,))]


def qkv_body(count, start, *refs):
    parts, (gain, cos, sin, w_far) = refs[:count], refs[count : count + 4]
    x_out, a_out, send, w_s, sems = refs[count + 4 :]
    copies = load_rows(w_far, slice(start, start + QKV_LANES), w_s, sems)
    x = parts[0][...].astype(F32)
    if count > 1:
        x = x + parts[1][...]
        for part in parts[2:]:
            x = x + unpack(part[...].astype(F32))
    low = x.astype(BF16)
    x_out[...] = low
    x = low.astype(F32)
    a = x * inverse_rms(x) * gain[...]
    for k in range(FSDP):
        a_out[k] = a[:, k * SHARD : (k + 1) * SHARD].astype(BF16)
    wait_all(copies)
    out = dot(a.astype(BF16), rows_of(w_s))
    qk = out[:, :QK_COLS]
    pairs = (HEADS + KV_HEADS) // 2
    lane = lax.broadcasted_iota(jnp.int32, qk.shape, 1)
    scale = jnp.where(lane < HEADS * HEAD, HEAD**-0.5, 1.0)
    cos_all = jnp.concatenate([cos[...]] * pairs, axis=1) * scale
    sin_all = jnp.concatenate([sin[...]] * pairs, axis=1) * scale
    qk = qk * cos_all + swap_halves(qk) * sin_all
    v = out[:, QK_COLS:QKV_COLS]
    for h in range(HEADS):
        g = h // GROUP
        q_h = qk[:, h * HEAD : (h + 1) * HEAD]
        k_g = qk[:, (HEADS + g) * HEAD : (HEADS + g + 1) * HEAD]
        v_g = v[:, g * HEAD : (g + 1) * HEAD]
        send[h, 0:ROWS] = jnp.concatenate([q_h, k_g], axis=1).astype(BF16)
        send[h, ROWS:] = pack(v_g).astype(BF16)
    for h in range(HEADS, CTX):
        send[h] = jnp.zeros(send.shape[1:], BF16)


def unpack_heads(recv, q_s, k_s, v_s):
    for b in range(2 * CTX):
        c, half = source_block(b)
        rows = slice(b * BLK, (b + 1) * BLK)
        qk = recv[c, half * BLK : (half + 1) * BLK, :].astype(F32)
        v = recv[c, ROWS : ROWS + BLK, :].astype(F32)
        q_s[rows, :] = qk[:, :HEAD].astype(BF16)
        k_s[rows, :] = qk[:, HEAD:].astype(BF16)
        v_s[rows, :] = v[:, half * HEAD : (half + 1) * HEAD].astype(BF16)


def masked_scores(q, keys, start):
    scores = dot_t(q, keys)
    row = lax.broadcasted_iota(jnp.int32, (TILE, TILE), 0)
    col = lax.broadcasted_iota(jnp.int32, (TILE, TILE), 1)
    last = jnp.where(col <= row, scores[:, start:], MASKED)
    return last if start == 0 else jnp.concatenate([scores[:, :start], last], axis=1)


def attend_body(recv, send, log_out, q_s, k_s, v_s, out_s):
    unpack_heads(recv, q_s, k_s, v_s)
    for i in range(LENGTH // TILE):
        start, stop = i * TILE, (i + 1) * TILE
        scores = masked_scores(q_s[start:stop, :], k_s[:stop, :], start)
        top = jnp.max(scores, axis=-1, keepdims=True)
        weights = jnp.exp(scores - top)
        total = jnp.sum(weights, axis=-1, keepdims=True)
        log_out[start:stop, :] = top + jnp.log(total)
        p = weights * (1.0 / total)
        out_s[start:stop, :] = dot(p.astype(BF16), v_s[:stop, :])
    for c in range(CTX):
        last = 2 * CTX - 1 - c
        pair = [out_s[c * BLK : (c + 1) * BLK, :], out_s[last * BLK : (last + 1) * BLK, :]]
        send[c] = jnp.concatenate(pair, axis=1).astype(BF16)


def mix_body(start, x, recv, gain, w_far, mixed_out, b_out, att_out, att_s, w_s, sems):
    copies = load_rows(w_far, slice(start, start + OUT_LANES), w_s, sems)
    for h in range(HEADS):
        pair = recv[h].astype(F32)
        cols = slice(h * HEAD, (h + 1) * HEAD)
        att_s[0:BLK, cols] = pair[:, :HEAD].astype(BF16)
        att_s[BLK:, cols] = pair[:, HEAD:].astype(BF16)
    att = att_s[...]
    for k in range(FSDP):
        att_out[k] = att_s[:, k * SHARD : (k + 1) * SHARD]
    wait_all(copies)
    mixed = x[...].astype(F32) + dot(att, rows_of(w_s))[:, :WIDTH]
    mixed_out[...] = mixed
    b_out[...] = pack(mixed * inverse_rms(mixed) * gain[...]).astype(BF16)


def spread(total, outs):
    outs[0][...] = total[0:ROWS]
    for k in range(1, FSDP):
        outs[k][...] = pack(total[k * ROWS : (k + 1) * ROWS]).astype(BF16)


def all_rows(parts):
    return jnp.concatenate([unpack(p[...]) for p in parts], axis=0)


def ffn_body(start, *refs):
    parts, w_far, (gate_out, up_out), outs = refs[:4], refs[4], refs[5:7], refs[7:11]
    w_s, sems, down_s, down_sem = refs[11:]
    copies = load_rows(w_far, slice(start, start + 2 * FF_SHARD), w_s, sems)
    down = load_down(w_far, slice(start + 2 * FF_SHARD, start + FFN_COLS), down_s, down_sem)
    rows = all_rows(parts)
    wait_all(copies)
    gate_up = dot(rows, rows_of(w_s))
    gate, up = gate_up[:, :FF_SHARD], gate_up[:, FF_SHARD:]
    gate_out[...] = gate
    up_out[...] = up
    hidden = (gate * jax.nn.sigmoid(gate) * up).astype(BF16)
    wait_all(down)
    spread(dot_t(hidden, rows_of(down_s)), outs)


def ffn_back_body(start, *refs):
    parts, (gate_ref, up_ref, w_far) = refs[:4], refs[4:7]
    hidden_out, d_gu_out = refs[7:9]
    outs = refs[9:13]
    w_s, sems, down_s, down_sem = refs[13:]
    down = load_down(w_far, slice(start + 2 * FF_SHARD, start + FFN_COLS), down_s, down_sem)
    copies = load_rows(w_far, slice(start, start + 2 * FF_SHARD), w_s, sems)
    rows = all_rows(parts)
    gate, up = gate_ref[...], up_ref[...]
    sig = jax.nn.sigmoid(gate)
    act = gate * sig
    hidden_out[...] = (act * up).astype(BF16)
    wait_all(down)
    d_hidden = dot(rows, rows_of(down_s))
    d_gu_out[:, :FF_SHARD] = (d_hidden * up * (sig * (1.0 + gate * (1.0 - sig)))).astype(BF16)
    d_gu_out[:, FF_SHARD:] = (d_hidden * act).astype(BF16)
    wait_all(copies)
    spread(dot_t(d_gu_out[...], rows_of(w_s)), outs)


def ffn_grad_body(*refs):
    b_parts, g_parts, d_gu, hidden, out = refs[:4], refs[4:8], refs[8], refs[9], refs[10]
    stage, sems = refs[11:]
    for c in range(SLICES, CTX):
        stage[c] = jnp.zeros(stage.shape[1:], BF16)
    rows = all_rows(b_parts)
    copies = []
    for group in range(3):
        lanes = slice(group * FF_SHARD, (group + 1) * FF_SHARD)
        if group < 2:
            grad = t_dot(rows, d_gu[:, lanes]).astype(BF16)
            for f in range(FSDP):
                for c in range(SLICES):
                    first = f * SHARD + c * SLICE
                    stage[c, f * SLICE : (f + 1) * SLICE, lanes] = grad[first : first + SLICE]
        else:
            grad = t_dot(all_rows(g_parts), hidden[...]).astype(BF16)
            for c in range(SLICES):
                stage[c, :, lanes] = grad[c * DOWN_SLICE : (c + 1) * DOWN_SLICE]
        copies.append(pltpu.make_async_copy(stage.at[:, :, lanes], out.at[:, :, lanes], sems.at[group]))
        copies[-1].start()
    wait_all(copies)


def mix_back_body(start, g, p0, p1, p2, p3, mixed, gain, w_far, d_mixed_out, ga_out, gain_out, send, w_s, sems):
    copies = load_rows(w_far, slice(start, start + OUT_LANES), w_s, sems)
    d_b = p0[...]
    for part in (p1, p2, p3):
        d_b = d_b + unpack(part[...].astype(F32))
    d_in, d_gain = norm_backward(d_b, mixed[...], gain[...])
    d_mixed = unpack(g[...].astype(F32)) + d_in
    d_mixed_out[...] = d_mixed
    gain_out[...] = d_gain
    ga_out[...] = pack(d_mixed).astype(BF16)
    wide = jnp.concatenate([d_mixed, jnp.zeros((ROWS, OUT_LANES - WIDTH), F32)], axis=1).astype(BF16)
    wait_all(copies)
    d_att = dot_t(wide, rows_of(w_s))
    for h in range(HEADS):
        send[h] = pack(d_att[:, h * HEAD : (h + 1) * HEAD]).astype(BF16)
    for h in range(HEADS, CTX):
        send[h] = jnp.zeros(send.shape[1:], BF16)


def attend_back_body(recv, d_recv, log_total, cos, sin, send, q_s, k_s, v_s, d_s, dq_s, dk_s, dv_s):
    unpack_heads(recv, q_s, k_s, v_s)
    for b in range(2 * CTX):
        c, half = source_block(b)
        pair = d_recv[c].astype(F32)
        d_s[b * BLK : (b + 1) * BLK, :] = pair[:, half * HEAD : (half + 1) * HEAD].astype(BF16)
    dk_s[...] = jnp.zeros(dk_s.shape, F32)
    dv_s[...] = jnp.zeros(dv_s.shape, F32)
    for i in range(LENGTH // TILE):
        start, stop = i * TILE, (i + 1) * TILE
        q, d_att = q_s[start:stop, :], d_s[start:stop, :]
        p = jnp.exp(masked_scores(q, k_s[:stop, :], start) - log_total[start:stop, :])
        d_p = dot_t(d_att, v_s[:stop, :])
        inner = jnp.sum(p * d_p, axis=-1, keepdims=True)
        d_scores = (p * (d_p - inner)).astype(BF16)
        dq_s[start:stop, :] = dot(d_scores, k_s[:stop, :])
        dk_s[:, :stop] += t_dot(q, d_scores)
        dv_s[:, :stop] += t_dot(d_att, p.astype(BF16))
    dk = dk_s[...].T
    dv = dv_s[...].T
    both = jnp.concatenate([dq_s[...] * (HEAD**-0.5), dk], axis=1)
    both = both * cos[...] - swap_halves(both) * sin[...]
    for c in range(CTX):
        last = 2 * CTX - 1 - c
        send[c, 0:BLK] = both[c * BLK : (c + 1) * BLK].astype(BF16)
        send[c, BLK:ROWS] = both[last * BLK : (last + 1) * BLK].astype(BF16)
        pair = [dv[c * BLK : (c + 1) * BLK], dv[last * BLK : (last + 1) * BLK]]
        send[c, ROWS:] = jnp.concatenate(pair, axis=1).astype(BF16)


def qkv_back_body(start, recv, d_mixed, x_ref, gain, gain_ffn, w_far, d_x_out, low_out, rows_out, rows_s, w_s, sems):
    copies = load_rows(w_far, slice(start, start + QKV_LANES), w_s, sems)
    rows_s[:, QKV_COLS:] = jnp.zeros((ROWS, QKV_LANES - QKV_COLS), BF16)
    for g in range(KV_HEADS):
        d_k = jnp.zeros((ROWS, HEAD), F32)
        d_v = jnp.zeros((BLK, 2 * HEAD), F32)
        for h in range(g * GROUP, (g + 1) * GROUP):
            qk = recv[h, 0:ROWS].astype(F32)
            rows_s[:, h * HEAD : (h + 1) * HEAD] = qk[:, :HEAD].astype(BF16)
            d_k = d_k + qk[:, HEAD:]
            d_v = d_v + recv[h, ROWS:].astype(F32)
        k_cols = slice((HEADS + g) * HEAD, (HEADS + g + 1) * HEAD)
        v_cols = slice(QK_COLS + g * HEAD, QK_COLS + (g + 1) * HEAD)
        rows_s[:, k_cols] = d_k.astype(BF16)
        rows_s[:, v_cols] = unpack(d_v).astype(BF16)
    rows = rows_s[...]
    rows_out[0:ROWS] = rows
    wait_all(copies)
    d_a = dot_t(rows, rows_of(w_s))
    d_in, d_gain = norm_backward(d_a, x_ref[...].astype(F32), gain[...])
    d_x = d_mixed[...] + d_in
    d_x_out[...] = d_x
    low_out[...] = pack(d_x).astype(BF16)
    gains = jnp.concatenate([d_gain, gain_ffn[...], jnp.zeros((SLICE - 2, WIDTH), F32)], axis=0)
    gains = jnp.concatenate([gains, jnp.zeros((SLICE, QKV_LANES - WIDTH), F32)], axis=1)
    rows_out[ROWS:] = gains.astype(BF16)


def qkv_grad_body(fsdp_ref, *refs):
    blocks, parts, others, out = refs[:4], refs[4:8], refs[8:-1], refs[-1]
    start = QKV_LANES
    for other in others:
        out[:, :, start : start + other.shape[2]] = other[...]
        start += other.shape[2]
    cols = jnp.concatenate([p[:, :SHARD] for p in blocks], axis=0)
    rows = jnp.concatenate([p[0:ROWS] for p in parts], axis=0)
    grad = t_dot(cols, rows).astype(BF16)
    for c in range(SLICES):
        out[by_core(c), :, :QKV_LANES] = grad[c * SLICE : (c + 1) * SLICE]
    gains = sum(p[ROWS:].astype(F32) for p in parts)
    mine = jnp.zeros((SLICE, SHARD), F32)
    for f in range(FSDP):
        mine = jnp.where(fsdp_ref[0] == f, gains[:, f * SHARD : (f + 1) * SHARD], mine)
    mine = jnp.concatenate([mine, jnp.zeros((SLICE, QKV_LANES - SHARD), F32)], axis=1)
    out[by_core(SLICES), :, :QKV_LANES] = mine.astype(BF16)


def out_grad_body(*refs):
    blocks, ga_parts, out = refs[:4], refs[4:8], refs[8]
    cols = jnp.concatenate([p[:, SHARD:] for p in blocks], axis=0)
    grad = t_dot(cols, all_rows(ga_parts))
    grad = jnp.concatenate([grad, jnp.zeros((SHARD, OUT_LANES - WIDTH), F32)], axis=1).astype(BF16)
    for c in range(SLICES):
        out[by_core(c)] = grad[c * SLICE : (c + 1) * SLICE]
    out[by_core(SLICES)] = jnp.zeros((SLICE, OUT_LANES), BF16)


def rest_result_body(fsdp_ref, gathered, gate, up, down, out):
    for c in range(SLICES):
        rows = slice(c * SLICE, (c + 1) * SLICE)
        for k in range(FSDP):
            member = lax.rem(fsdp_ref[0] + FSDP - k, FSDP)
            cols = pl.ds(pl.multiple_of(member * FF_SHARD, 128), FF_SHARD)
            piece = gathered[c, k * SLICE : (k + 1) * SLICE, : 2 * FF_SHARD].astype(F32)
            gate[rows, cols] = piece[:, :FF_SHARD]
            up[rows, cols] = piece[:, FF_SHARD:]
        out[rows] = gathered[c, FSDP * SLICE :, :WIDTH].astype(F32)
        down[c * DOWN_SLICE : (c + 1) * DOWN_SLICE] = gathered[c, 0 : FSDP * SLICE, 2 * FF_SHARD : FFN_COLS].astype(F32)


def qkv_result_body(core_ref, same, other, query, key, value, gains, kv_s):
    kv = KV_HEADS * HEAD
    swapped = core_ref[0] == 1
    gathered = []
    for c in range(CTX):
        here, there = (same, other) if c % 2 == 0 else (other, same)
        gathered.append(jnp.where(swapped, there[c // 2], here[c // 2]))
    for c in range(SLICES):
        rows = slice(c * SLICE, (c + 1) * SLICE)
        piece = gathered[c].astype(F32)
        query[rows] = piece[:, :WIDTH]
        kv_s[rows] = piece[:, WIDTH:QKV_COLS]
    turned = kv_s[...].T
    key[...] = turned[:kv]
    value[...] = turned[kv:]
    gains[...] = gathered[SLICES][:8, :SHARD].astype(F32)


def shifted(x, axis, distance):
    n = lax.axis_size(axis)
    return lax.ppermute(x, axis, [(i, (i + distance) % n) for i in range(n)])


def around(x):
    return [x] + [shifted(x, "fsdp", k) for k in range(1, FSDP)]


def back_around(parts):
    return [parts[0]] + [shifted(parts[k], "fsdp", -k) for k in range(1, FSDP)]


def exchange_blocks(blocks, index):
    pick = lambda k: lax.dynamic_index_in_dim(blocks, (index + k) % FSDP, 0, keepdims=False)
    return [pick(0)] + [shifted(pick(k), "fsdp", k) for k in range(1, FSDP)]


def swap_sections(x):
    return lax.ppermute(x, "section", [(0, 1), (1, 0)])


def all_to_all(x, axis):
    return lax.all_to_all(x, axis, 0, 0)


def after(x, *earlier):
    return lax.optimization_barrier((x, earlier))[0]


def core_pair(x):
    return lax.ppermute(x, "ctx", [(i, i ^ 1) for i in range(CTX)])


def same_core(x):
    return lax.all_to_all(x, "ctx", 0, 0, axis_index_groups=[list(range(k, CTX, 2)) for k in range(2)])


def to_all(x, axis, count):
    return all_to_all(jnp.broadcast_to(x[None], (count,) + x.shape), axis)


def on_device(
    tokens,
    cotangent,
    norm_attn,
    w_query,
    key_projection,
    value_projection,
    w_out,
    norm_ffn,
    w_gate,
    w_up,
    w_down,
):
    section = lax.axis_index("section")
    ctx = lax.axis_index("ctx")
    fsdp = lax.axis_index("fsdp")
    first = section == 0

    place = jnp.minimum(ctx, SLICES - 1)

    def my_slice(rows, count=SLICE):
        return lax.dynamic_slice_in_dim(rows, place * count, count, 0)

    own_gains = jnp.concatenate([norm_attn, norm_ffn], axis=1)
    own_gains = jnp.pad(own_gains, ((0, SLICE - 1), (0, QKV_LANES + OUT_LANES - 2 * SHARD)))
    own = [my_slice(w[0]) for w in (w_query, key_projection, value_projection)]
    own.append(jnp.zeros((SLICE, QKV_LANES - QKV_COLS), BF16))
    own += [my_slice(w_out[0]), jnp.zeros((SLICE, OUT_LANES - WIDTH), BF16)]
    own = jnp.where(ctx < SLICES, jnp.concatenate(own, axis=1), own_gains)
    attention = to_all(own, ("section", "fsdp"), 2 * FSDP).reshape(2, FSDP * SLICE, QKV_LANES + OUT_LANES)

    ffn = [my_slice(w[0]).reshape(SLICE, FSDP, FF_SHARD) for w in (w_gate, w_up)]
    ffn = jnp.concatenate(ffn, axis=2).transpose(1, 0, 2)
    ffn = all_to_all(after(jnp.concatenate([ffn, ffn]), attention), ("section", "fsdp"))
    ffn = ffn.reshape(2, FSDP * SLICE, 2 * FF_SHARD)
    down = my_slice(w_down[0].T, DOWN_SLICE)
    down_other = swap_sections(after(down, attention))
    downs = (jnp.where(first, down, down_other), jnp.where(first, down_other, down))
    ffn = [jnp.concatenate(pair, axis=1) for pair in zip(ffn, downs)]

    gathered = lax.all_gather(attention[0], "ctx")
    qkv_weights, out_weights = [(gathered, 0)], [(gathered, QKV_LANES)]
    ffn_weights = []

    def gains_of(layer):
        source, start = qkv_weights[layer]
        rows = source[SLICES, ::SLICE, start : start + 2 * SHARD].astype(F32)
        return rows[:, :SHARD].reshape(1, WIDTH), rows[:, SHARD:].reshape(1, WIDTH)

    cos_all, sin_all = rotary_constants()
    cos_all, sin_all = jnp.asarray(cos_all), jnp.asarray(sin_all)

    def own_positions(table):
        pieces = [
            lax.dynamic_slice_in_dim(table, start * BLK, BLK, 0) for start in (ctx, 2 * CTX - 1 - ctx)
        ]
        return jnp.concatenate(pieces)

    cos_own, sin_own = own_positions(cos_all), own_positions(sin_all)

    def mine(x):
        return lax.dynamic_index_in_dim(x, section, 0, keepdims=False).reshape(2, BLK, WIDTH)

    my_rows = mine(tokens).reshape(ROWS, WIDTH)
    my_cotangent = mine(cotangent).transpose(1, 0, 2).reshape(BLK, 2 * WIDTH)

    row_f32, row_bf16 = sds((ROWS, WIDTH), F32), sds((ROWS, WIDTH), BF16)
    packed = sds((BLK, 2 * WIDTH), BF16)
    heads_shape = sds((CTX, ROWS + BLK, 2 * HEAD), BF16)
    att_shape = sds((CTX, BLK, 2 * HEAD), BF16)
    blocks_shape = sds((FSDP, ROWS, SHARD), BF16)
    seq = lambda dtype: pltpu.VMEM((LENGTH, HEAD), dtype)
    partials = [row_f32] + [packed] * 3
    ff_f32, ff_bf16 = sds((FSDP * ROWS, FF_SHARD), F32), sds((FSDP * ROWS, FF_SHARD), BF16)
    qkv_scratch, out_scratch = row_scratch(QKV_LANES), row_scratch(OUT_LANES)
    ffn_scratch = row_scratch(2 * FF_SHARD) + [
        pltpu.VMEM((SLICES, DOWN_SLICE, FF_SHARD), BF16), pltpu.SemaphoreType.DMA,
    ]
    bind = functools.partial

    kept = []
    parts = [my_rows]
    for layer in range(2):
        qkv_w, qkv_at = qkv_weights[layer]
        gain_attn, gain_ffn = gains_of(layer)
        x, a_blocks, send = call(
            bind(qkv_body, len(parts), qkv_at), [row_bf16, blocks_shape, heads_shape],
            *parts, gain_attn, cos_own, sin_own, far=[qkv_w],
            scratch=qkv_scratch, flops=2 * ROWS * WIDTH * QKV_COLS,
        )
        if layer == 0:
            gathered = jnp.concatenate([ffn[0], attention[1][:, :QKV_LANES]], axis=1)
            gathered = lax.all_gather(gathered, "ctx")
            ffn_weights.append((gathered, 0))
            qkv_weights.append((gathered, FFN_COLS))
        heads = all_to_all(send, "ctx")
        beside = []
        if layer == 1:
            first_blocks = exchange_blocks(after(kept[0][1], send), fsdp)
            beside = first_blocks
        send, log_total = call(
            attend_body, [att_shape, sds((LENGTH, 1), F32)], heads,
            wait_for=beside, scratch=[seq(BF16), seq(BF16), seq(BF16), seq(F32)], flops=2 * LENGTH * LENGTH * HEAD,
        )
        arrived = all_to_all(send, "ctx")
        if layer == 0:
            gathered = jnp.concatenate([ffn[1], attention[1][:, QKV_LANES:]], axis=1)
            gathered = lax.all_gather(after(gathered, arrived), "ctx")
            ffn_weights.append((gathered, 0))
            out_weights.append((gathered, FFN_COLS))
        (out_w, out_at), (ffn_w, ffn_at) = out_weights[layer], ffn_weights[layer]
        mixed, b, att_blocks = call(
            bind(mix_body, out_at), [row_f32, packed, blocks_shape],
            x, arrived, gain_ffn, far=[out_w],
            scratch=[pltpu.VMEM((ROWS, WIDTH), BF16)] + out_scratch, flops=2 * ROWS * WIDTH * WIDTH,
        )
        b_all = around(b)
        gate, up, *outs = call(
            bind(ffn_body, ffn_at), [ff_f32, ff_f32] + partials, *b_all, far=[ffn_w],
            scratch=ffn_scratch, flops=2 * FSDP * ROWS * WIDTH * FF_SHARD * 3,
        )
        if layer == 0:
            parts = [mixed] + back_around(outs)
        blocks = jnp.concatenate([a_blocks, att_blocks], axis=2)
        kept.append((x, blocks, heads, log_total, mixed, b_all, gate, up, gain_attn, gain_ffn))
    first_acts, last_outs = kept[1][0], outs

    g = my_cotangent
    ffn_grads, out_grads, d_inputs = [None, None], [None, None], [None, None]
    fsdp_index = fsdp.astype(jnp.int32).reshape(1)

    def ffn_gradient(b_all, g_all, d_gu, hidden):
        slices = call(
            ffn_grad_body, [sds((CTX, FSDP * SLICE, FFN_COLS), BF16)], *b_all, *g_all, d_gu, hidden, far_out=True,
            scratch=[pltpu.VMEM((CTX, FSDP * SLICE, FFN_COLS), BF16), pltpu.SemaphoreType.DMA((3,))],
            flops=2 * FSDP * ROWS * WIDTH * FFN_COLS,
        )[0]
        return slices.reshape(CTX * FSDP * SLICE, FFN_COLS)

    def qkv_gradient(blocks, d_rows, *others, wait_for=()):
        lanes = QKV_LANES + sum(other.shape[2] for other in others)
        return call(
            qkv_grad_body, [sds((CTX, SLICE, lanes), BF16)], fsdp_index, *blocks, *d_rows, *others,
            wait_for=wait_for, scalars=1, flops=2 * FSDP * ROWS * SHARD * QKV_COLS,
        )[0]

    def out_gradient(blocks, ga):
        return call(
            out_grad_body, [sds((CTX, SLICE, OUT_LANES), BF16)], *blocks, *ga,
            flops=2 * FSDP * ROWS * SHARD * WIDTH,
        )[0]

    def reduced(slices):
        halves = slices.reshape(2, CTX // 2, *slices.shape[1:])
        keep, give = [lax.dynamic_index_in_dim(halves, k, 0, keepdims=False) for k in (ctx % 2, 1 - ctx % 2)]
        half = (keep.astype(F32) + core_pair(give).astype(F32)).astype(BF16)
        return same_core(half).astype(F32).sum(axis=0).astype(BF16)

    for layer in (1, 0):
        x, blocks, heads, log_total, mixed, b_all, gate, up, gain_attn, gain_ffn = kept[layer]
        (qkv_w, qkv_at), (out_w, out_at), (ffn_w, ffn_at) = qkv_weights[layer], out_weights[layer], ffn_weights[layer]
        g_all = around(g)
        hidden, d_gu, *outs = call(
            bind(ffn_back_body, ffn_at),
            [ff_bf16, sds((FSDP * ROWS, 2 * FF_SHARD), BF16)] + partials,
            *g_all, gate, up, far=[ffn_w],
            scratch=ffn_scratch, flops=2 * FSDP * ROWS * WIDTH * FF_SHARD * 3,
        )
        arrived = back_around(outs)
        slices = ffn_gradient(b_all, g_all, d_gu, hidden)
        ffn_grads[layer] = lax.psum_scatter(slices, "ctx", scatter_dimension=0, tiled=True)
        d_mixed, ga, d_gain_ffn, send = call(
            bind(mix_back_body, out_at), [row_f32, packed, sds((1, WIDTH), F32), att_shape],
            g, *arrived, mixed, gain_ffn, far=[out_w], wait_for=[slices],
            scratch=out_scratch, flops=2 * ROWS * WIDTH * WIDTH,
        )
        if layer == 1:
            ga = around(after(ga, send))
            beside = ga
        else:
            late_rows = around(after(d_rows, send))
            last_acts = kept[1][4] + last_parts[0]
            for part in last_parts[1:]:
                part = part.reshape(BLK, 2, WIDTH).transpose(1, 0, 2).reshape(ROWS, WIDTH)
                last_acts = last_acts + part.astype(F32)
            last_acts = last_acts.astype(BF16)
            other_acts = swap_sections(after(jnp.where(first, last_acts, first_acts), send))
            beside = [*late_rows, other_acts]
        send = call(
            attend_back_body, [heads_shape],
            heads, all_to_all(send, "ctx"), log_total, cos_all, sin_all,
            scratch=[seq(BF16)] * 4 + [seq(F32)] + [pltpu.VMEM((HEAD, LENGTH), F32)] * 2,
            flops=5 * LENGTH * LENGTH * HEAD,
        )[0]
        send = after(send, *beside)
        if layer == 1:
            blocks = exchange_blocks(after(blocks, send), fsdp)
            last_parts = back_around([after(part, send) for part in last_outs])
            out_grads[1] = out_gradient(blocks, ga)
            beside, late_blocks = [*last_parts, out_grads[1]], blocks
        else:
            blocks = first_blocks
            ga = around(after(ga, send))
            late_slices = qkv_gradient(late_blocks, late_rows)
            out_grads[0] = out_gradient(blocks, ga)
            beside = [late_slices, out_grads[0]]
        d_x, d_low, d_rows = call(
            bind(qkv_back_body, qkv_at),
            [row_f32, packed, sds((ROWS + SLICE, QKV_LANES), BF16)],
            all_to_all(send, "ctx"), d_mixed, x, gain_attn, d_gain_ffn, far=[qkv_w], wait_for=beside,
            scratch=[pltpu.VMEM((ROWS, QKV_LANES), BF16)] + qkv_scratch,
            flops=2 * ROWS * WIDTH * QKV_COLS,
        )
        d_inputs[layer] = (d_x, d_low)
        g = d_low

    def across(zero, one):
        keep, give = jnp.where(first, zero, one), jnp.where(first, one, zero)
        return (keep.astype(F32) + swap_sections(give).astype(F32)).astype(BF16)

    late_slices = reduced(after(jnp.concatenate([late_slices, *out_grads], axis=2), d_rows))
    d_rows = around(d_rows)
    ffn_slices = across(*[after(grad, d_rows[0]) for grad in ffn_grads])
    gate_up = ffn_slices[:, : 2 * FF_SHARD].reshape(FSDP, SLICE, 2 * FF_SHARD)
    gate_up = jnp.concatenate(exchange_blocks(gate_up, fsdp))
    ffn_slices = jnp.concatenate([gate_up, ffn_slices[:, 2 * FF_SHARD :]], axis=1)
    slices = qkv_gradient(blocks, d_rows, wait_for=[late_slices, ffn_slices])
    out_grads = [late_slices[:, start : start + OUT_LANES] for start in (QKV_LANES, QKV_LANES + OUT_LANES)]
    out_slices = across(*[after(grad, *d_rows[1:]) for grad in out_grads])
    out_slices = jnp.pad(out_slices, ((0, 0), (0, FFN_COLS - OUT_LANES)))
    rest_slices = jnp.concatenate([ffn_slices, out_slices])
    other_grads = swap_sections(after(jnp.where(first, d_inputs[1][1], d_inputs[0][1]), slices))
    qkv_slices = across(reduced(slices), late_slices[:, :QKV_LANES])
    gate, up, down, out = call(
        rest_result_body,
        [sds((SHARD, FF), F32), sds((SHARD, FF), F32), sds((WIDTH, FF_SHARD), F32), sds((SHARD, WIDTH), F32)],
        fsdp_index, lax.all_gather(rest_slices, "ctx"), scalars=1,
    )
    kv = KV_HEADS * HEAD
    qkv_same = same_core(jnp.broadcast_to(qkv_slices[None], (CTX // 2,) + qkv_slices.shape))
    query, key, value, gains = call(
        qkv_result_body,
        [sds((SHARD, WIDTH), F32), sds((kv, SHARD), F32), sds((kv, SHARD), F32), sds((8, SHARD), F32)],
        (ctx % 2).astype(jnp.int32).reshape(1), qkv_same, core_pair(qkv_same),
        scratch=[pltpu.VMEM((SHARD, 2 * kv), F32)], scalars=1, wait_for=[gate, other_grads],
    )
    other_grads = other_grads.reshape(BLK, 2, WIDTH).transpose(1, 0, 2).reshape(ROWS, WIDTH).astype(F32)
    d_one = d_inputs[1][1].reshape(BLK, 2, WIDTH).transpose(1, 0, 2).reshape(ROWS, WIDTH).astype(F32)
    mine_grads = jnp.where(first, d_inputs[0][0], d_one)
    mine_acts = jnp.where(first, first_acts, last_acts)

    def by_micro(own, other):
        pair = jnp.stack([jnp.where(first, own, other), jnp.where(first, other, own)])
        return pair.reshape(1, 2, 1, 2, BLK, WIDTH)

    return (
        by_micro(mine_acts, other_acts),
        by_micro(mine_grads, other_grads),
        gains[0:1],
        query[None],
        key.T[None],
        value.T[None],
        out[None],
        gains[1:2],
        gate[None],
        up[None],
        down.T[None],
    )


def solution(mesh):
    rows = P(None, "fsdp", None, "ctx", None)
    gain, matrix = P("section", "fsdp"), P("section", "fsdp", None)
    layer_rows = P("section", None, "fsdp", None, "ctx", None)
    weights = (gain, matrix, matrix, matrix, matrix, gain, matrix, matrix, matrix)
    return jax.shard_map(
        on_device,
        mesh=mesh,
        in_specs=(rows, rows) + weights,
        out_specs=(layer_rows, layer_rows) + weights,
        check_vma=False,
    )
```
